32 devices in a mesh: pb: 8 (over y, x, core), ga: 4 (over z).
Axes of the slice: x: 2, y: 2, z: 4, core: 2. Of those that a mesh axis runs over, the one named last changes fastest.
Arguments:
- elements: bfloat16 [8, 64, 112, 2048], P('pb', None, None, 'ga'), may hold values from -0.75 to 0.75
- screened: bfloat16 [8, 2048, 2048], P('pb', 'ga'), may hold values from -0.125 to 0.125
- counts: int32 [8], P('pb'), may hold values from 1536 to 2048
- k_minus_q: int32 [8], P('pb'), may hold values from 0 to 575
- occupation: float32 [576, 64], replicated, may hold values from 0.25 to 1
Outputs:
- sigma: float32 [112, 112], P('ga')
The draws below stay inside these ranges and needn't reach their ends.
Inputs may be any that keep to these rules, and one draw needn't show every extreme that they name: counts[q] G-vectors, the leading ones, lie inside the sphere of q. k_minus_q[q] is a row of occupation.
All inputs are finite; a program needn't handle non-finite values.
Results may differ from the reference program's by a relative error of at most 0.0029.
Values may be sent and summed in bfloat16 or wider, within the bound.
A program may use at most 128 MiB of HBM per device.

```python
import jax
import jax.numpy as jnp
from jax import lax

G = 2048
S = 112
V = 64
NB = 32
KPTS = 576
Q = 8
N_GA = 4


def set_ends(drawn, own_key, smallest, largest):
    longest = drawn.shape.index(max(drawn.shape))
    spots = []
    for shift in (0, 1):
        where = [jax.random.randint(jax.random.fold_in(own_key, axis), (), 0, length) for axis, length in enumerate(drawn.shape)]
        where[longest] = (where[longest] + shift) % drawn.shape[longest]
        spots.append(tuple(where))
    return drawn.at[spots[0]].set(smallest).at[spots[1]].set(largest)


def levels(stream_key, dims, split, low, largest):
    factor_of = 1.0
    for axis_at, shards_of in split:
        steps = jax.random.uniform(jax.random.fold_in(jax.random.fold_in(stream_key, 6), axis_at), (shards_of,), jnp.float32, low / len(split), largest / len(split))
        factor_of = factor_of * jnp.repeat(jnp.exp(steps), dims[axis_at] // shards_of).reshape((-1,) + (1,) * (len(dims) - 1 - axis_at))
    return factor_of


def normal_values(own_key, dims, spread, bound, cuts=(), held_as=jnp.bfloat16):
    gain = levels(own_key, dims, cuts, -0.22, 0.18) if cuts else 1.0
    drawn = jax.random.normal(own_key, dims, jnp.float32) * spread * gain
    return jnp.minimum(jnp.maximum(drawn, -bound), bound).astype(held_as)


def setup_inputs(seed: int = 0) -> dict:
    key_of = jax.random.split(jax.random.key(seed), 6)
    elements = normal_values(key_of[0], (Q, V, S, G), (1.0 / (G * V) ** 0.25), 0.75, ((0, 8), (3, 4)))
    screened = normal_values(key_of[1], (Q, G, G), G ** -0.5, 0.125, ((0, 8), (1, 4)))
    counts = set_ends(jax.random.randint(key_of[2], (Q,), 3 * G // 4, G + 1), jax.random.fold_in(key_of[2], 1), 3 * G // 4, G).astype(jnp.int32)
    k_minus_q = set_ends(jax.random.randint(key_of[3], (Q,), 0, KPTS), jax.random.fold_in(key_of[3], 1), 0, KPTS - 1).astype(jnp.int32)
    occupation = jnp.clip(jax.random.uniform(key_of[4], (KPTS, V), jnp.float32, 0.25, 1.0), 0.25, 1.0)
    return {"elements": elements, "screened": screened, "counts": counts, "k_minus_q": k_minus_q, "occupation": occupation}


def reference(elements, screened, counts, k_minus_q, occupation):
    n_cycles = G // (N_GA * NB)
    g_index = jnp.arange(G, dtype=jnp.int32)
    k_index = jnp.arange(KPTS, dtype=jnp.int32)

    def single_q(inputs):
        element_q, stored_q, sphere_count, k_point = inputs
        w_true = stored_q.reshape(N_GA, n_cycles, NB, G).transpose(1, 0, 2, 3).reshape(G, G)
        inside = (g_index < sphere_count).astype(jnp.bfloat16)
        masked = element_q * inside[None, None, :]
        product = jnp.dot(masked.reshape(V * S, G), w_true, preferred_element_type=jnp.float32)
        product = product.astype(jnp.bfloat16).reshape(V, S, G)
        weights = jnp.sum(jnp.where((k_index == k_point)[:, None], occupation, jnp.float32(0.0)), axis=0)
        pair_terms = jnp.einsum("vmg,vng->vmn", product.astype(jnp.float32), masked.astype(jnp.float32), precision=lax.Precision.HIGHEST)
        return -jnp.einsum("v,vmn->mn", weights, pair_terms, precision=lax.Precision.HIGHEST)

    per_q = lax.map(single_q, (elements, screened, counts, k_minus_q))
    return jnp.sum(per_q, axis=0)
```

```python
import functools

import jax
import jax.numpy as jnp
from jax import lax
from jax.experimental import pallas as pl
from jax.experimental.pallas import tpu as pltpu
from jax.sharding import PartitionSpec as P

NB = 32
MESH = pl.DeviceIdType.MESH


def kernel(
    n, n_pb, vg, wc,
    elements, screened, counts, k_minus_q, occupation, out,
    mbuf, wbuf, wown, occ, pair, acc, parts, ga_in, pb_in,
    local_sem, wsend, wrecv, msend, mrecv, gsend, grecv, psend, precv,
):
    me = lax.axis_index("ga")
    my_pb = lax.axis_index("pb")
    _, v_per, n_state, g_slab = elements.shape
    n_cycles, _, g_total = screened.shape
    rows = n_state // n
    nk = v_per // vg
    nc = n_cycles // wc

    def peer(offset):
        return lax.rem(me + offset, n)

    def pb_peer(offset):
        return lax.rem(my_pb + offset, n_pb)

    my_lanes = pl.ds(pl.multiple_of(me * g_slab, g_slab), g_slab)
    own_w = pltpu.make_async_copy(screened, wown, local_sem.at[0])
    own_m = pltpu.make_async_copy(elements.at[me], mbuf.at[:, :, my_lanes], local_sem.at[1])
    own_occ = pltpu.make_async_copy(occupation, occ, local_sem.at[2])
    own_w.start()
    own_m.start()
    own_occ.start()

    barrier = pltpu.get_barrier_semaphore()
    for offset in range(1, n):
        pl.semaphore_signal(barrier, inc=1, device_id={"ga": peer(offset)}, device_id_type=MESH)
    for offset in range(1, n_pb):
        pl.semaphore_signal(barrier, inc=1, device_id={"pb": pb_peer(offset)}, device_id_type=MESH)
    pl.semaphore_wait(barrier, n - 1 + n_pb - 1)

    def m_copy(k, offset):
        return pltpu.make_async_remote_copy(
            src_ref=elements.at[peer(offset), pl.ds(k * vg, vg)],
            dst_ref=mbuf.at[pl.ds(k * vg, vg), :, my_lanes],
            send_sem=msend.at[offset - 1, k],
            recv_sem=mrecv.at[offset - 1, k],
            device_id={"ga": peer(offset)},
            device_id_type=MESH,
        )

    def w_copy(source, chunk, step):
        side = 0 if step < 0 else 1
        return pltpu.make_async_remote_copy(
            src_ref=wbuf.at[pl.ds(chunk * wc, wc), source],
            dst_ref=wbuf.at[pl.ds(chunk * wc, wc), source],
            send_sem=wsend.at[side, source, chunk],
            recv_sem=wrecv.at[source, chunk],
            device_id={"ga": lax.rem(me + step + n, n)},
            device_id_type=MESH,
        )

    started = []

    def send_next_m():
        if len(started) < nk:
            for offset in range(n - 1, 0, -1):
                m_copy(len(started), offset).start()
            started.append(0)

    own_w.wait()
    count = counts[0]
    column = lax.broadcasted_iota(jnp.int32, (NB, g_total), 1)
    row = lax.broadcasted_iota(jnp.int32, (NB, g_total), 0)

    for chunk in range(nc):

        def mask_block(c, carry):
            g = row + (c * n + me) * NB
            inside = jnp.logical_and(g < count, column < count)
            block = wown[c].astype(jnp.float32)
            wbuf[c, me] = jnp.where(inside, block, 0.0).astype(jnp.bfloat16)
            return carry

        lax.fori_loop(chunk * wc, (chunk + 1) * wc, mask_block, 0)

        @pl.when(me > 0)
        def _():
            w_copy(me, chunk, -1).start()

        @pl.when(me < n - 1)
        def _():
            w_copy(me, chunk, 1).start()

        if chunk == 0:
            send_next_m()

    for distance in range(1, n):
        for chunk in range(nc):
            source = me - distance

            @pl.when(source >= 0)
            def _():
                w_copy(source, chunk, 1).wait_recv()

                @pl.when(me < n - 1)
                def _():
                    w_copy(source, chunk, 1).start()

            source_up = me + distance

            @pl.when(source_up < n)
            def _():
                w_copy(source_up, chunk, -1).wait_recv()

                @pl.when(me > 0)
                def _():
                    w_copy(source_up, chunk, -1).start()

            send_next_m()
    while len(started) < nk:
        send_next_m()

    own_m.wait()
    own_occ.wait()
    weights = occ[pl.ds(k_minus_q[0], 1), :]
    band = lax.broadcasted_iota(jnp.int32, weights.shape, 1)
    acc[...] = jnp.zeros_like(acc)
    ht = min(512, g_total)

    def group(k, carry):
        for offset in range(1, n):
            m_copy(k, offset).wait_recv()
        pair[...] = jnp.zeros_like(pair)

        def tile(h, inner):
            lanes = pl.ds(pl.multiple_of(h * ht, ht), ht)
            left = mbuf[pl.ds(k * vg, vg)].reshape(vg * n_state, g_total)
            w = wbuf[:, :, :, lanes].reshape(g_total, ht)
            product = jnp.dot(left, w, preferred_element_type=jnp.float32).astype(jnp.bfloat16)
            for v in range(vg):
                pair[v] += lax.dot_general(
                    product[v * n_state : (v + 1) * n_state],
                    mbuf[k * vg + v, :, lanes],
                    (((1,), (1,)), ((), ())),
                    preferred_element_type=jnp.float32,
                )
            return inner

        lax.fori_loop(0, g_total // ht, tile, 0)
        for v in range(vg):
            here = band == me * v_per + k * vg + v
            weight = jnp.sum(jnp.where(here, weights, 0.0), axis=1, keepdims=True)
            acc[...] -= weight * pair[v]
        return carry

    lax.fori_loop(0, nk, group, 0)

    def g_copy(offset):
        return pltpu.make_async_remote_copy(
            src_ref=parts.at[peer(offset)],
            dst_ref=ga_in.at[me],
            send_sem=gsend.at[offset - 1],
            recv_sem=grecv.at[offset - 1],
            device_id={"ga": peer(offset)},
            device_id_type=MESH,
        )

    parts[...] = jnp.zeros_like(parts)
    for j in range(n):
        parts[j, 0:rows, 0:n_state] = acc[j * rows : (j + 1) * rows, :]
    for offset in range(1, n):
        g_copy(offset).start()
    ga_in[me] = parts[me]
    for offset in range(1, n):
        g_copy(offset).wait_recv()
    total = ga_in[0]
    for j in range(1, n):
        total = total + ga_in[j]
    pb_in[my_pb] = total

    def p_copy(offset):
        return pltpu.make_async_remote_copy(
            src_ref=pb_in.at[my_pb],
            dst_ref=pb_in.at[my_pb],
            send_sem=psend.at[offset - 1],
            recv_sem=precv.at[offset - 1],
            device_id={"pb": pb_peer(offset)},
            device_id_type=MESH,
        )

    for offset in range(1, n_pb):
        p_copy(offset).start()
    for offset in range(1, n_pb):
        p_copy(offset).wait_recv()
    result = pb_in[0]
    for j in range(1, n_pb):
        result = result + pb_in[j]
    out[...] = result[0:rows, 0:n_state]

    for offset in range(1, n_pb):
        p_copy(offset).wait_send()
    for offset in range(1, n):
        g_copy(offset).wait_send()
        for k in range(nk):
            m_copy(k, offset).wait_send()
    for source in range(n):
        for chunk in range(nc):

            @pl.when(jnp.logical_and(me > 0, source >= me))
            def _():
                w_copy(source, chunk, -1).wait_send()

            @pl.when(jnp.logical_and(me < n - 1, source <= me))
            def _():
                w_copy(source, chunk, 1).wait_send()


def on_device(n, n_pb, elements, screened, counts, k_minus_q, occupation):
    _, n_band, n_state, g_slab = elements.shape
    g_total = screened.shape[2]
    v_per = n_band // n
    n_cycles = g_slab // NB
    vg = 2 if v_per % 2 == 0 else 1
    nc = min(4, n_cycles)
    wc = n_cycles // nc
    nk = v_per // vg
    rows = n_state // n
    padded = (rows + 7) // 8 * 8
    lanes = (n_state + 127) // 128 * 128
    any_spec = pl.BlockSpec(memory_space=pl.ANY)
    smem = pl.BlockSpec(memory_space=pltpu.SMEM)
    vmem = pl.BlockSpec(memory_space=pltpu.VMEM)
    dma = pltpu.SemaphoreType.DMA
    return pl.pallas_call(
        functools.partial(kernel, n, n_pb, vg, wc),
        out_shape=jax.ShapeDtypeStruct((rows, n_state), jnp.float32),
        in_specs=[any_spec, any_spec, smem, smem, any_spec],
        out_specs=vmem,
        scratch_shapes=[
            pltpu.VMEM((v_per, n_state, g_total), jnp.bfloat16),
            pltpu.VMEM((n_cycles, n, NB, g_total), jnp.bfloat16),
            pltpu.VMEM((n_cycles, NB, g_total), jnp.bfloat16),
            pltpu.VMEM(occupation.shape, jnp.float32),
            pltpu.VMEM((vg, n_state, n_state), jnp.float32),
            pltpu.VMEM((n_state, n_state), jnp.float32),
            pltpu.VMEM((n, padded, lanes), jnp.float32),
            pltpu.VMEM((n, padded, lanes), jnp.float32),
            pltpu.VMEM((n_pb, padded, lanes), jnp.float32),
            dma((3,)),
            dma((2, n, nc)),
            dma((n, nc)),
            dma((n - 1, nk)),
            dma((n - 1, nk)),
            dma((n - 1,)),
            dma((n - 1,)),
            dma((n_pb - 1,)),
            dma((n_pb - 1,)),
        ],
        compiler_params=pltpu.CompilerParams(
            collective_id=0, has_side_effects=True, vmem_limit_bytes=48 * 1024 * 1024
        ),
        cost_estimate=pl.CostEstimate(
            flops=2 * v_per * n_state * g_total * (g_total + n_state),
            bytes_accessed=16 * 1024 * 1024,
            transcendentals=0,
        ),
    )(
        elements.reshape(n, v_per, n_state, g_slab),
        screened.reshape(n_cycles, NB, g_total),
        counts,
        k_minus_q,
        occupation,
    )


def solution(mesh):
    return jax.shard_map(
        functools.partial(on_device, mesh.shape["ga"], mesh.shape["pb"]),
        mesh=mesh,
        in_specs=(P("pb", None, None, "ga"), P("pb", "ga", None), P("pb"), P("pb"), P()),
        out_specs=P("ga", None),
        check_vma=False,
    )
```

```python
import functools

import jax
import jax.numpy as jnp
from jax import lax
from jax.experimental import pallas as pl
from jax.experimental.pallas import tpu as pltpu
from jax.sharding import PartitionSpec as P

NB = 32
MESH = pl.DeviceIdType.MESH


def kernel(
    n, n_pb, vg, wc,
    elements, screened, counts, k_minus_q, occupation, out,
    mbuf, wbuf, wown, occ, pair, acc, parts, ga_in, pb_in,
    local_sem, wsend, wrecv, msend, mrecv, gsend, grecv, psend, precv,
):
    me = lax.axis_index("ga")
    my_pb = lax.axis_index("pb")
    _, v_per, n_state, g_slab = elements.shape
    n_cycles, _, g_total = screened.shape
    rows = n_state // n
    nk = v_per // vg
    nc = n_cycles // wc

    def peer(offset):
        return lax.rem(me + offset, n)

    def pb_peer(offset):
        return lax.rem(my_pb + offset, n_pb)

    my_lanes = pl.ds(pl.multiple_of(me * g_slab, g_slab), g_slab)
    own_w = pltpu.make_async_copy(screened, wown, local_sem.at[0])
    own_m = pltpu.make_async_copy(elements.at[me], mbuf.at[:, :, my_lanes], local_sem.at[1])
    own_occ = pltpu.make_async_copy(occupation, occ, local_sem.at[2])
    own_w.start()
    own_m.start()
    own_occ.start()

    barrier = pltpu.get_barrier_semaphore()
    for offset in range(1, n):
        pl.semaphore_signal(barrier, inc=1, device_id={"ga": peer(offset)}, device_id_type=MESH)
    for offset in range(1, n_pb):
        pl.semaphore_signal(barrier, inc=1, device_id={"pb": pb_peer(offset)}, device_id_type=MESH)
    pl.semaphore_wait(barrier, n - 1 + n_pb - 1)

    def m_copy(k, offset):
        return pltpu.make_async_remote_copy(
            src_ref=elements.at[peer(offset), pl.ds(k * vg, vg)],
            dst_ref=mbuf.at[pl.ds(k * vg, vg), :, my_lanes],
            send_sem=msend.at[offset - 1, k],
            recv_sem=mrecv.at[offset - 1, k],
            device_id={"ga": peer(offset)},
            device_id_type=MESH,
        )

    def w_copy(source, chunk, step):
        side = 0 if step < 0 else 1
        return pltpu.make_async_remote_copy(
            src_ref=wbuf.at[pl.ds(chunk * wc, wc), source],
            dst_ref=wbuf.at[pl.ds(chunk * wc, wc), source],
            send_sem=wsend.at[side, source, chunk],
            recv_sem=wrecv.at[source, chunk],
            device_id={"ga": lax.rem(me + step + n, n)},
            device_id_type=MESH,
        )

    started = []

    def is_end(offset):
        return jnp.logical_or(peer(offset) == 0, peer(offset) == n - 1)

    def send_next_m():
        if len(started) < nk:
            k = len(started)
            for offset in range(1, n):

                @pl.when(jnp.logical_not(is_end(offset)))
                def _():
                    m_copy(k, offset).start()

            started.append(0)

    own_w.wait()
    count = counts[0]
    column = lax.broadcasted_iota(jnp.int32, (NB, g_total), 1)
    row = lax.broadcasted_iota(jnp.int32, (NB, g_total), 0)

    for chunk in range(nc):

        def mask_block(c, carry):
            g = row + (c * n + me) * NB
            inside = jnp.logical_and(g < count, column < count)
            block = wown[c].astype(jnp.float32)
            wbuf[c, me] = jnp.where(inside, block, 0.0).astype(jnp.bfloat16)
            return carry

        lax.fori_loop(chunk * wc, (chunk + 1) * wc, mask_block, 0)

        @pl.when(me > 0)
        def _():
            w_copy(me, chunk, -1).start()

        @pl.when(me < n - 1)
        def _():
            w_copy(me, chunk, 1).start()

        if chunk == 0:
            send_next_m()

    for distance in range(1, n):
        for chunk in range(nc):
            source = me - distance

            @pl.when(source >= 0)
            def _():
                w_copy(source, chunk, 1).wait_recv()

                @pl.when(me < n - 1)
                def _():
                    w_copy(source, chunk, 1).start()

            source_up = me + distance

            @pl.when(source_up < n)
            def _():
                w_copy(source_up, chunk, -1).wait_recv()

                @pl.when(me > 0)
                def _():
                    w_copy(source_up, chunk, -1).start()

            send_next_m()
    while len(started) < nk:
        send_next_m()
    for k in range(nk):
        for offset in range(1, n):

            @pl.when(is_end(offset))
            def _():
                m_copy(k, offset).start()

    own_m.wait()
    own_occ.wait()
    weights = occ[pl.ds(k_minus_q[0], 1), :]
    band = lax.broadcasted_iota(jnp.int32, weights.shape, 1)
    acc[...] = jnp.zeros_like(acc)
    ht = min(512, g_total)

    def group(k, carry):
        for offset in range(1, n):
            m_copy(k, offset).wait_recv()
        pair[...] = jnp.zeros_like(pair)

        def tile(h, inner):
            lanes = pl.ds(pl.multiple_of(h * ht, ht), ht)
            left = mbuf[pl.ds(k * vg, vg)].reshape(vg * n_state, g_total)
            w = wbuf[:, :, :, lanes].reshape(g_total, ht)
            product = jnp.dot(left, w, preferred_element_type=jnp.float32).astype(jnp.bfloat16)
            for v in range(vg):
                pair[v] += lax.dot_general(
                    product[v * n_state : (v + 1) * n_state],
                    mbuf[k * vg + v, :, lanes],
                    (((1,), (1,)), ((), ())),
                    preferred_element_type=jnp.float32,
                )
            return inner

        lax.fori_loop(0, g_total // ht, tile, 0)
        for v in range(vg):
            here = band == me * v_per + k * vg + v
            weight = jnp.sum(jnp.where(here, weights, 0.0), axis=1, keepdims=True)
            acc[...] -= weight * pair[v]
        return carry

    lax.fori_loop(0, nk, group, 0)

    def g_copy(offset):
        return pltpu.make_async_remote_copy(
            src_ref=parts.at[peer(offset)],
            dst_ref=ga_in.at[me],
            send_sem=gsend.at[offset - 1],
            recv_sem=grecv.at[offset - 1],
            device_id={"ga": peer(offset)},
            device_id_type=MESH,
        )

    parts[...] = jnp.zeros_like(parts)
    for j in range(n):
        parts[j, 0:rows, 0:n_state] = acc[j * rows : (j + 1) * rows, :]
    for offset in range(1, n):
        g_copy(offset).start()
    ga_in[me] = parts[me]
    for offset in range(1, n):
        g_copy(offset).wait_recv()
    total = ga_in[0]
    for j in range(1, n):
        total = total + ga_in[j]
    pb_in[my_pb] = total

    def p_copy(offset):
        return pltpu.make_async_remote_copy(
            src_ref=pb_in.at[my_pb],
            dst_ref=pb_in.at[my_pb],
            send_sem=psend.at[offset - 1],
            recv_sem=precv.at[offset - 1],
            device_id={"pb": pb_peer(offset)},
            device_id_type=MESH,
        )

    for offset in range(1, n_pb):
        p_copy(offset).start()
    for offset in range(1, n_pb):
        p_copy(offset).wait_recv()
    result = pb_in[0]
    for j in range(1, n_pb):
        result = result + pb_in[j]
    out[...] = result[0:rows, 0:n_state]

    for offset in range(1, n_pb):
        p_copy(offset).wait_send()
    for offset in range(1, n):
        g_copy(offset).wait_send()
        for k in range(nk):
            m_copy(k, offset).wait_send()
    for source in range(n):
        for chunk in range(nc):

            @pl.when(jnp.logical_and(me > 0, source >= me))
            def _():
                w_copy(source, chunk, -1).wait_send()

            @pl.when(jnp.logical_and(me < n - 1, source <= me))
            def _():
                w_copy(source, chunk, 1).wait_send()


def on_device(n, n_pb, elements, screened, counts, k_minus_q, occupation):
    _, n_band, n_state, g_slab = elements.shape
    g_total = screened.shape[2]
    v_per = n_band // n
    n_cycles = g_slab // NB
    vg = 2 if v_per % 2 == 0 else 1
    nc = min(4, n_cycles)
    wc = n_cycles // nc
    nk = v_per // vg
    rows = n_state // n
    padded = (rows + 7) // 8 * 8
    lanes = (n_state + 127) // 128 * 128
    any_spec = pl.BlockSpec(memory_space=pl.ANY)
    smem = pl.BlockSpec(memory_space=pltpu.SMEM)
    vmem = pl.BlockSpec(memory_space=pltpu.VMEM)
    dma = pltpu.SemaphoreType.DMA
    return pl.pallas_call(
        functools.partial(kernel, n, n_pb, vg, wc),
        out_shape=jax.ShapeDtypeStruct((rows, n_state), jnp.float32),
        in_specs=[any_spec, any_spec, smem, smem, any_spec],
        out_specs=vmem,
        scratch_shapes=[
            pltpu.VMEM((v_per, n_state, g_total), jnp.bfloat16),
            pltpu.VMEM((n_cycles, n, NB, g_total), jnp.bfloat16),
            pltpu.VMEM((n_cycles, NB, g_total), jnp.bfloat16),
            pltpu.VMEM(occupation.shape, jnp.float32),
            pltpu.VMEM((vg, n_state, n_state), jnp.float32),
            pltpu.VMEM((n_state, n_state), jnp.float32),
            pltpu.VMEM((n, padded, lanes), jnp.float32),
            pltpu.VMEM((n, padded, lanes), jnp.float32),
            pltpu.VMEM((n_pb, padded, lanes), jnp.float32),
            dma((3,)),
            dma((2, n, nc)),
            dma((n, nc)),
            dma((n - 1, nk)),
            dma((n - 1, nk)),
            dma((n - 1,)),
            dma((n - 1,)),
            dma((n_pb - 1,)),
            dma((n_pb - 1,)),
        ],
        compiler_params=pltpu.CompilerParams(
            collective_id=0, has_side_effects=True, vmem_limit_bytes=48 * 1024 * 1024
        ),
        cost_estimate=pl.CostEstimate(
            flops=2 * v_per * n_state * g_total * (g_total + n_state),
            bytes_accessed=16 * 1024 * 1024,
            transcendentals=0,
        ),
    )(
        elements.reshape(n, v_per, n_state, g_slab),
        screened.reshape(n_cycles, NB, g_total),
        counts,
        k_minus_q,
        occupation,
    )


def solution(mesh):
    return jax.shard_map(
        functools.partial(on_device, mesh.shape["ga"], mesh.shape["pb"]),
        mesh=mesh,
        in_specs=(P("pb", None, None, "ga"), P("pb", "ga", None), P("pb"), P("pb"), P()),
        out_specs=P("ga", None),
        check_vma=False,
    )
```

```python
import functools

import jax
import jax.numpy as jnp
from jax import lax
from jax.experimental import pallas as pl
from jax.experimental.pallas import tpu as pltpu
from jax.sharding import PartitionSpec as P

NB = 32
MESH = pl.DeviceIdType.MESH


def kernel(
    n, n_pb, vg, wc,
    elements, screened, counts, k_minus_q, occupation, out,
    mbuf, wbuf, wown, occ, pair, acc, parts, ga_in, pb_in,
    local_sem, wsend, wrecv, msend, mrecv, gsend, grecv, psend, precv,
):
    me = lax.axis_index("ga")
    my_pb = lax.axis_index("pb")
    _, v_per, n_state, g_slab = elements.shape
    n_cycles, _, g_total = screened.shape
    rows = n_state // n
    nk = v_per // vg
    nc = n_cycles // wc

    def peer(offset):
        return lax.rem(me + offset, n)

    def pb_peer(offset):
        return lax.rem(my_pb + offset, n_pb)

    own_w = pltpu.make_async_copy(screened, wown, local_sem.at[0])
    own_m = pltpu.make_async_copy(elements.at[me], mbuf.at[me], local_sem.at[1])
    own_occ = pltpu.make_async_copy(occupation, occ, local_sem.at[2])
    own_w.start()
    own_m.start()
    own_occ.start()

    barrier = pltpu.get_barrier_semaphore()
    for offset in range(1, n):
        pl.semaphore_signal(barrier, inc=1, device_id={"ga": peer(offset)}, device_id_type=MESH)
    for offset in range(1, n_pb):
        pl.semaphore_signal(barrier, inc=1, device_id={"pb": pb_peer(offset)}, device_id_type=MESH)
    pl.semaphore_wait(barrier, n - 1 + n_pb - 1)

    def m_copy(k, offset):
        return pltpu.make_async_remote_copy(
            src_ref=elements.at[peer(offset), pl.ds(k * vg, vg)],
            dst_ref=mbuf.at[me, pl.ds(k * vg, vg)],
            send_sem=msend.at[offset - 1, k],
            recv_sem=mrecv.at[offset - 1, k],
            device_id={"ga": peer(offset)},
            device_id_type=MESH,
        )

    def w_copy(source, chunk, step):
        side = 0 if step < 0 else 1
        return pltpu.make_async_remote_copy(
            src_ref=wbuf.at[pl.ds(chunk * wc, wc), source],
            dst_ref=wbuf.at[pl.ds(chunk * wc, wc), source],
            send_sem=wsend.at[side, source, chunk],
            recv_sem=wrecv.at[source, chunk],
            device_id={"ga": lax.rem(me + step + n, n)},
            device_id_type=MESH,
        )

    started = []

    def send_next_m():
        if len(started) < nk:
            for offset in range(n - 1, 0, -1):
                m_copy(len(started), offset).start()
            started.append(0)

    own_w.wait()
    count = counts[0]
    column = lax.broadcasted_iota(jnp.int32, (NB, g_total), 1)
    row = lax.broadcasted_iota(jnp.int32, (NB, g_total), 0)

    for chunk in range(nc):

        def mask_block(c, carry):
            g = row + (c * n + me) * NB
            inside = jnp.logical_and(g < count, column < count)
            block = wown[c].astype(jnp.float32)
            wbuf[c, me] = jnp.where(inside, block, 0.0).astype(jnp.bfloat16)
            return carry

        lax.fori_loop(chunk * wc, (chunk + 1) * wc, mask_block, 0)

        @pl.when(me > 0)
        def _():
            w_copy(me, chunk, -1).start()

        @pl.when(me < n - 1)
        def _():
            w_copy(me, chunk, 1).start()

        if chunk == 0:
            send_next_m()

    for distance in range(1, n):
        for chunk in range(nc):
            source = me - distance

            @pl.when(source >= 0)
            def _():
                w_copy(source, chunk, 1).wait_recv()

                @pl.when(me < n - 1)
                def _():
                    w_copy(source, chunk, 1).start()

            source_up = me + distance

            @pl.when(source_up < n)
            def _():
                w_copy(source_up, chunk, -1).wait_recv()

                @pl.when(me > 0)
                def _():
                    w_copy(source_up, chunk, -1).start()

            send_next_m()
    while len(started) < nk:
        send_next_m()

    own_m.wait()
    own_occ.wait()
    weights = occ[pl.ds(k_minus_q[0], 1), :]
    band = lax.broadcasted_iota(jnp.int32, weights.shape, 1)
    acc[...] = jnp.zeros_like(acc)

    def group(k, carry):
        for offset in range(1, n):
            m_copy(k, offset).wait_recv()
        pair[...] = jnp.zeros_like(pair)

        def tile(h, inner):
            lanes = pl.ds(pl.multiple_of(h * g_slab, g_slab), g_slab)
            left = jnp.concatenate(
                [mbuf[a, pl.ds(k * vg, vg)].reshape(vg * n_state, g_slab) for a in range(n)], axis=1
            )
            w = wbuf[:, :, :, lanes].reshape(g_total, g_slab)
            product = jnp.dot(left, w, preferred_element_type=jnp.float32).astype(jnp.bfloat16)
            for v in range(vg):
                pair[v] += lax.dot_general(
                    product[v * n_state : (v + 1) * n_state],
                    mbuf[h, k * vg + v],
                    (((1,), (1,)), ((), ())),
                    preferred_element_type=jnp.float32,
                )
            return inner

        lax.fori_loop(0, n, tile, 0)
        for v in range(vg):
            here = band == me * v_per + k * vg + v
            weight = jnp.sum(jnp.where(here, weights, 0.0), axis=1, keepdims=True)
            acc[...] -= weight * pair[v]
        return carry

    lax.fori_loop(0, nk, group, 0)

    def g_copy(offset):
        return pltpu.make_async_remote_copy(
            src_ref=parts.at[peer(offset)],
            dst_ref=ga_in.at[me],
            send_sem=gsend.at[offset - 1],
            recv_sem=grecv.at[offset - 1],
            device_id={"ga": peer(offset)},
            device_id_type=MESH,
        )

    parts[...] = jnp.zeros_like(parts)
    for j in range(n):
        parts[j, 0:rows, 0:n_state] = acc[j * rows : (j + 1) * rows, :]
    for offset in range(1, n):
        g_copy(offset).start()
    ga_in[me] = parts[me]
    for offset in range(1, n):
        g_copy(offset).wait_recv()
    total = ga_in[0]
    for j in range(1, n):
        total = total + ga_in[j]
    pb_in[my_pb] = total

    def p_copy(offset):
        return pltpu.make_async_remote_copy(
            src_ref=pb_in.at[my_pb],
            dst_ref=pb_in.at[my_pb],
            send_sem=psend.at[offset - 1],
            recv_sem=precv.at[offset - 1],
            device_id={"pb": pb_peer(offset)},
            device_id_type=MESH,
        )

    for offset in range(1, n_pb):
        p_copy(offset).start()
    for offset in range(1, n_pb):
        p_copy(offset).wait_recv()
    result = pb_in[0]
    for j in range(1, n_pb):
        result = result + pb_in[j]
    out[...] = result[0:rows, 0:n_state]

    for offset in range(1, n_pb):
        p_copy(offset).wait_send()
    for offset in range(1, n):
        g_copy(offset).wait_send()
        for k in range(nk):
            m_copy(k, offset).wait_send()
    for source in range(n):
        for chunk in range(nc):

            @pl.when(jnp.logical_and(me > 0, source >= me))
            def _():
                w_copy(source, chunk, -1).wait_send()

            @pl.when(jnp.logical_and(me < n - 1, source <= me))
            def _():
                w_copy(source, chunk, 1).wait_send()


def on_device(n, n_pb, elements, screened, counts, k_minus_q, occupation):
    _, n_band, n_state, g_slab = elements.shape
    g_total = screened.shape[2]
    v_per = n_band // n
    n_cycles = g_slab // NB
    vg = 2 if v_per % 2 == 0 else 1
    nc = min(4, n_cycles)
    wc = n_cycles // nc
    nk = v_per // vg
    rows = n_state // n
    padded = (rows + 7) // 8 * 8
    lanes = (n_state + 127) // 128 * 128
    any_spec = pl.BlockSpec(memory_space=pl.ANY)
    smem = pl.BlockSpec(memory_space=pltpu.SMEM)
    vmem = pl.BlockSpec(memory_space=pltpu.VMEM)
    dma = pltpu.SemaphoreType.DMA
    return pl.pallas_call(
        functools.partial(kernel, n, n_pb, vg, wc),
        out_shape=jax.ShapeDtypeStruct((rows, n_state), jnp.float32),
        in_specs=[any_spec, any_spec, smem, smem, any_spec],
        out_specs=vmem,
        scratch_shapes=[
            pltpu.VMEM((n, v_per, n_state, g_slab), jnp.bfloat16),
            pltpu.VMEM((n_cycles, n, NB, g_total), jnp.bfloat16),
            pltpu.VMEM((n_cycles, NB, g_total), jnp.bfloat16),
            pltpu.VMEM(occupation.shape, jnp.float32),
            pltpu.VMEM((vg, n_state, n_state), jnp.float32),
            pltpu.VMEM((n_state, n_state), jnp.float32),
            pltpu.VMEM((n, padded, lanes), jnp.float32),
            pltpu.VMEM((n, padded, lanes), jnp.float32),
            pltpu.VMEM((n_pb, padded, lanes), jnp.float32),
            dma((3,)),
            dma((2, n, nc)),
            dma((n, nc)),
            dma((n - 1, nk)),
            dma((n - 1, nk)),
            dma((n - 1,)),
            dma((n - 1,)),
            dma((n_pb - 1,)),
            dma((n_pb - 1,)),
        ],
        compiler_params=pltpu.CompilerParams(
            collective_id=0, has_side_effects=True, vmem_limit_bytes=48 * 1024 * 1024
        ),
        cost_estimate=pl.CostEstimate(
            flops=2 * v_per * n_state * g_total * (g_total + n_state),
            bytes_accessed=16 * 1024 * 1024,
            transcendentals=0,
        ),
    )(
        elements.reshape(n, v_per, n_state, g_slab),
        screened.reshape(n_cycles, NB, g_total),
        counts,
        k_minus_q,
        occupation,
    )


def solution(mesh):
    return jax.shard_map(
        functools.partial(on_device, mesh.shape["ga"], mesh.shape["pb"]),
        mesh=mesh,
        in_specs=(P("pb", None, None, "ga"), P("pb", "ga", None), P("pb"), P("pb"), P()),
        out_specs=P("ga", None),
        check_vma=False,
    )
```

```python
import functools

import jax
import jax.numpy as jnp
from jax import lax
from jax.experimental import pallas as pl
from jax.experimental.pallas import tpu as pltpu
from jax.sharding import PartitionSpec as P

NB = 32
MESH = pl.DeviceIdType.MESH


def kernel(
    n, n_pb, vg, wc,
    elements, screened, counts, k_minus_q, occupation, out,
    mbuf, wbuf, wown, occ, pair, acc, parts, ga_in, pb_in,
    local_sem, wsend, wrecv, msend, mrecv, gsend, grecv, psend, precv,
):
    me = lax.axis_index("ga")
    my_pb = lax.axis_index("pb")
    _, v_per, n_state, g_slab = elements.shape
    n_cycles, _, g_total = screened.shape
    rows = n_state // n
    nk = v_per // vg
    nc = n_cycles // wc

    def peer(offset):
        return lax.rem(me + offset, n)

    def pb_peer(offset):
        return lax.rem(my_pb + offset, n_pb)

    own_w = pltpu.make_async_copy(screened, wown, local_sem.at[0])
    own_m = pltpu.make_async_copy(elements.at[me], mbuf.at[me, me], local_sem.at[1])
    own_occ = pltpu.make_async_copy(occupation, occ, local_sem.at[2])
    own_w.start()
    own_m.start()
    own_occ.start()

    barrier = pltpu.get_barrier_semaphore()
    for offset in range(1, n):
        pl.semaphore_signal(barrier, inc=1, device_id={"ga": peer(offset)}, device_id_type=MESH)
    for offset in range(1, n_pb):
        pl.semaphore_signal(barrier, inc=1, device_id={"pb": pb_peer(offset)}, device_id_type=MESH)
    pl.semaphore_wait(barrier, n - 1 + n_pb - 1)

    def hop(src, source, target, k, step):
        here = (source, target, pl.ds(k * vg, vg))
        return pltpu.make_async_remote_copy(
            src_ref=mbuf.at[here] if src is None else src.at[target, pl.ds(k * vg, vg)],
            dst_ref=mbuf.at[here],
            send_sem=msend.at[source, target, k],
            recv_sem=mrecv.at[source, target, k],
            device_id={"ga": lax.rem(me + step + n, n)},
            device_id_type=MESH,
        )

    def w_copy(source, chunk, step):
        side = 0 if step < 0 else 1
        return pltpu.make_async_remote_copy(
            src_ref=wbuf.at[pl.ds(chunk * wc, wc), source],
            dst_ref=wbuf.at[pl.ds(chunk * wc, wc), source],
            send_sem=wsend.at[side, source, chunk],
            recv_sem=wrecv.at[source, chunk],
            device_id={"ga": lax.rem(me + step + n, n)},
            device_id_type=MESH,
        )

    own_w.wait()
    count = counts[0]
    column = lax.broadcasted_iota(jnp.int32, (NB, g_total), 1)
    row = lax.broadcasted_iota(jnp.int32, (NB, g_total), 0)

    for chunk in range(nc):

        def mask_block(c, carry):
            g = row + (c * n + me) * NB
            inside = jnp.logical_and(g < count, column < count)
            block = wown[c].astype(jnp.float32)
            wbuf[c, me] = jnp.where(inside, block, 0.0).astype(jnp.bfloat16)
            return carry

        lax.fori_loop(chunk * wc, (chunk + 1) * wc, mask_block, 0)

        @pl.when(me > 0)
        def _():
            w_copy(me, chunk, -1).start()

        @pl.when(me < n - 1)
        def _():
            w_copy(me, chunk, 1).start()

    def own_elements(i, carry):
        reach = n - 1 - i // nk
        k = lax.rem(i, nk)

        @pl.when(me - reach >= 0)
        def _():
            hop(elements, me, me - reach, k, -1).start()

        @pl.when(me + reach < n)
        def _():
            hop(elements, me, me + reach, k, 1).start()

        return carry

    lax.fori_loop(0, (n - 1) * nk, own_elements, 0)

    def round_of(distance, carry):
        low = me - distance
        high = me + distance

        def pass_w(chunk, inner):
            @pl.when(low >= 0)
            def _():
                w_copy(low, chunk, 1).wait_recv()

                @pl.when(me < n - 1)
                def _():
                    w_copy(low, chunk, 1).start()

            @pl.when(high < n)
            def _():
                w_copy(high, chunk, -1).wait_recv()

                @pl.when(me > 0)
                def _():
                    w_copy(high, chunk, -1).start()

            return inner

        lax.fori_loop(0, nc, pass_w, 0)

        def pass_m(i, inner):
            reach = n - 1 - i // nk
            k = lax.rem(i, nk)

            @pl.when(jnp.logical_and(low >= 0, me + reach < n))
            def _():
                hop(None, low, me + reach, k, 1).wait_recv()
                hop(None, low, me + reach, k, 1).start()

            @pl.when(jnp.logical_and(high < n, me - reach >= 0))
            def _():
                hop(None, high, me - reach, k, -1).wait_recv()
                hop(None, high, me - reach, k, -1).start()

            return inner

        lax.fori_loop(0, (n - 1) * nk, pass_m, 0)
        return carry

    lax.fori_loop(1, n, round_of, 0)

    own_m.wait()
    own_occ.wait()
    weights = occ[pl.ds(k_minus_q[0], 1), :]
    band = lax.broadcasted_iota(jnp.int32, weights.shape, 1)
    acc[...] = jnp.zeros_like(acc)

    def group(k, carry):
        for source in range(n):

            @pl.when(source != me)
            def _():
                hop(None, source, me, k, 1).wait_recv()

        pair[...] = jnp.zeros_like(pair)

        def tile(h, inner):
            lanes = pl.ds(pl.multiple_of(h * g_slab, g_slab), g_slab)
            left = jnp.concatenate(
                [mbuf[a, me, pl.ds(k * vg, vg)].reshape(vg * n_state, g_slab) for a in range(n)], axis=1
            )
            w = wbuf[:, :, :, lanes].reshape(g_total, g_slab)
            product = jnp.dot(left, w, preferred_element_type=jnp.float32).astype(jnp.bfloat16)
            for v in range(vg):
                pair[v] += lax.dot_general(
                    product[v * n_state : (v + 1) * n_state],
                    mbuf[h, me, k * vg + v],
                    (((1,), (1,)), ((), ())),
                    preferred_element_type=jnp.float32,
                )
            return inner

        lax.fori_loop(0, n, tile, 0)
        for v in range(vg):
            here = band == me * v_per + k * vg + v
            weight = jnp.sum(jnp.where(here, weights, 0.0), axis=1, keepdims=True)
            acc[...] -= weight * pair[v]
        return carry

    lax.fori_loop(0, nk, group, 0)

    def g_copy(offset):
        return pltpu.make_async_remote_copy(
            src_ref=parts.at[peer(offset)],
            dst_ref=ga_in.at[me],
            send_sem=gsend.at[offset - 1],
            recv_sem=grecv.at[offset - 1],
            device_id={"ga": peer(offset)},
            device_id_type=MESH,
        )

    parts[...] = jnp.zeros_like(parts)
    for j in range(n):
        parts[j, 0:rows, 0:n_state] = acc[j * rows : (j + 1) * rows, :]
    for offset in range(1, n):
        g_copy(offset).start()
    ga_in[me] = parts[me]
    for offset in range(1, n):
        g_copy(offset).wait_recv()
    total = ga_in[0]
    for j in range(1, n):
        total = total + ga_in[j]
    pb_in[my_pb] = total

    def p_copy(offset):
        return pltpu.make_async_remote_copy(
            src_ref=pb_in.at[my_pb],
            dst_ref=pb_in.at[my_pb],
            send_sem=psend.at[offset - 1],
            recv_sem=precv.at[offset - 1],
            device_id={"pb": pb_peer(offset)},
            device_id_type=MESH,
        )

    for offset in range(1, n_pb):
        p_copy(offset).start()
    for offset in range(1, n_pb):
        p_copy(offset).wait_recv()
    result = pb_in[0]
    for j in range(1, n_pb):
        result = result + pb_in[j]
    out[...] = result[0:rows, 0:n_state]

    for offset in range(1, n_pb):
        p_copy(offset).wait_send()
    for offset in range(1, n):
        g_copy(offset).wait_send()

    def sent_elements(i, carry):
        source = i // (n * nk)
        target = lax.rem(i // nk, n)
        k = lax.rem(i, nk)

        @pl.when(jnp.logical_and(source == me, target != me))
        def _():
            hop(elements, source, target, k, 1).wait_send()

        passed = jnp.logical_or(
            jnp.logical_and(source < me, target > me), jnp.logical_and(source > me, target < me)
        )

        @pl.when(passed)
        def _():
            hop(None, source, target, k, 1).wait_send()

        return carry

    lax.fori_loop(0, n * n * nk, sent_elements, 0)
    for source in range(n):
        for chunk in range(nc):

            @pl.when(jnp.logical_and(me > 0, source >= me))
            def _():
                w_copy(source, chunk, -1).wait_send()

            @pl.when(jnp.logical_and(me < n - 1, source <= me))
            def _():
                w_copy(source, chunk, 1).wait_send()


def on_device(n, n_pb, elements, screened, counts, k_minus_q, occupation):
    _, n_band, n_state, g_slab = elements.shape
    g_total = screened.shape[2]
    v_per = n_band // n
    n_cycles = g_slab // NB
    vg = 4 if v_per % 4 == 0 else 1
    nc = min(4, n_cycles)
    wc = n_cycles // nc
    nk = v_per // vg
    rows = n_state // n
    padded = (rows + 7) // 8 * 8
    lanes = (n_state + 127) // 128 * 128
    any_spec = pl.BlockSpec(memory_space=pl.ANY)
    smem = pl.BlockSpec(memory_space=pltpu.SMEM)
    vmem = pl.BlockSpec(memory_space=pltpu.VMEM)
    dma = pltpu.SemaphoreType.DMA
    return pl.pallas_call(
        functools.partial(kernel, n, n_pb, vg, wc),
        out_shape=jax.ShapeDtypeStruct((rows, n_state), jnp.float32),
        in_specs=[any_spec, any_spec, smem, smem, any_spec],
        out_specs=vmem,
        scratch_shapes=[
            pltpu.VMEM((n, n, v_per, n_state, g_slab), jnp.bfloat16),
            pltpu.VMEM((n_cycles, n, NB, g_total), jnp.bfloat16),
            pltpu.VMEM((n_cycles, NB, g_total), jnp.bfloat16),
            pltpu.VMEM(occupation.shape, jnp.float32),
            pltpu.VMEM((vg, n_state, n_state), jnp.float32),
            pltpu.VMEM((n_state, n_state), jnp.float32),
            pltpu.VMEM((n, padded, lanes), jnp.float32),
            pltpu.VMEM((n, padded, lanes), jnp.float32),
            pltpu.VMEM((n_pb, padded, lanes), jnp.float32),
            dma((3,)),
            dma((2, n, nc)),
            dma((n, nc)),
            dma((n, n, nk)),
            dma((n, n, nk)),
            dma((n - 1,)),
            dma((n - 1,)),
            dma((n_pb - 1,)),
            dma((n_pb - 1,)),
        ],
        compiler_params=pltpu.CompilerParams(
            collective_id=0, has_side_effects=True, vmem_limit_bytes=56 * 1024 * 1024
        ),
        cost_estimate=pl.CostEstimate(
            flops=2 * v_per * n_state * g_total * (g_total + n_state),
            bytes_accessed=16 * 1024 * 1024,
            transcendentals=0,
        ),
    )(
        elements.reshape(n, v_per, n_state, g_slab),
        screened.reshape(n_cycles, NB, g_total),
        counts,
        k_minus_q,
        occupation,
    )


def solution(mesh):
    return jax.shard_map(
        functools.partial(on_device, mesh.shape["ga"], mesh.shape["pb"]),
        mesh=mesh,
        in_specs=(P("pb", None, None, "ga"), P("pb", "ga", None), P("pb"), P("pb"), P()),
        out_specs=P("ga", None),
        check_vma=False,
    )
```

```python
import functools

import jax
import jax.numpy as jnp
from jax import lax
from jax.experimental import pallas as pl
from jax.experimental.pallas import tpu as pltpu
from jax.sharding import PartitionSpec as P

NB = 32
MESH = pl.DeviceIdType.MESH


def kernel(
    n, n_pb, vg, wc,
    elements, screened, counts, k_minus_q, occupation, out,
    mbuf, wbuf, wown, occ, prod, pair, acc, parts, ga_in, pb_in,
    local_sem, wsend, wrecv, msend, mrecv, gsend, grecv, psend, precv,
):
    me = lax.axis_index("ga")
    my_pb = lax.axis_index("pb")
    _, v_per, n_state, g_slab = elements.shape
    n_cycles, _, g_total = screened.shape
    rows = n_state // n
    nk = v_per // vg
    nc = n_cycles // wc

    def peer(offset):
        return lax.rem(me + offset, n)

    def pb_peer(offset):
        return lax.rem(my_pb + offset, n_pb)

    own_w = pltpu.make_async_copy(screened, wown, local_sem.at[0])
    own_m = pltpu.make_async_copy(elements, mbuf.at[me], local_sem.at[1])
    own_occ = pltpu.make_async_copy(occupation, occ, local_sem.at[2])
    own_w.start()
    own_m.start()
    own_occ.start()

    barrier = pltpu.get_barrier_semaphore()
    for offset in range(1, n):
        pl.semaphore_signal(barrier, inc=1, device_id={"ga": peer(offset)}, device_id_type=MESH)
    for offset in range(1, n_pb):
        pl.semaphore_signal(barrier, inc=1, device_id={"pb": pb_peer(offset)}, device_id_type=MESH)
    pl.semaphore_wait(barrier, n - 1 + n_pb - 1)

    def hop(src, source, target, k, step):
        here = (source, target, pl.ds(k * vg, vg))
        return pltpu.make_async_remote_copy(
            src_ref=mbuf.at[here] if src is None else src.at[target, pl.ds(k * vg, vg)],
            dst_ref=mbuf.at[here],
            send_sem=msend.at[source, target, k],
            recv_sem=mrecv.at[source, target, k],
            device_id={"ga": lax.rem(me + step + n, n)},
            device_id_type=MESH,
        )

    def lanes_of(h):
        return pl.ds(pl.multiple_of(h * g_slab, g_slab), g_slab)

    def first_slab(chunk):
        return chunk * wc * n * NB // g_slab

    def last_slab(chunk):
        return ((chunk + 1) * wc * n * NB - 1) // g_slab

    def reaches_left(chunk, h, device):
        return jnp.logical_or(first_slab(chunk) <= device, h <= device)

    def reaches_right(chunk, h, device):
        return jnp.logical_or(last_slab(chunk) >= device, h >= device)

    def w_copy(source, chunk, h, step):
        side = 0 if step < 0 else 1
        piece = chunk * n + h
        here = (pl.ds(chunk * wc, wc), source, slice(None), lanes_of(h))
        return pltpu.make_async_remote_copy(
            src_ref=wbuf.at[here],
            dst_ref=wbuf.at[here],
            send_sem=wsend.at[side, source, piece],
            recv_sem=wrecv.at[source, piece],
            device_id={"ga": lax.rem(me + step + n, n)},
            device_id_type=MESH,
        )

    def goes_left(chunk, h):
        return jnp.logical_and(me > 0, reaches_left(chunk, h, me - 1))

    def goes_right(chunk, h):
        return jnp.logical_and(me < n - 1, reaches_right(chunk, h, me + 1))

    own_w.wait()
    count = counts[0]
    column = lax.broadcasted_iota(jnp.int32, (NB, g_total), 1)
    row = lax.broadcasted_iota(jnp.int32, (NB, g_total), 0)

    for chunk in range(nc):

        def mask_block(c, carry):
            g = row + (c * n + me) * NB
            inside = jnp.logical_and(g < count, column < count)
            block = wown[c].astype(jnp.float32)
            wbuf[c, me] = jnp.where(inside, block, 0.0).astype(jnp.bfloat16)
            return carry

        lax.fori_loop(chunk * wc, (chunk + 1) * wc, mask_block, 0)

        def send_own(h, carry):
            @pl.when(goes_left(chunk, h))
            def _():
                w_copy(me, chunk, h, -1).start()

            @pl.when(goes_right(chunk, h))
            def _():
                w_copy(me, chunk, h, 1).start()

            return carry

        lax.fori_loop(0, n, send_own, 0)

    def own_elements(i, carry):
        reach = n - 1 - i // nk
        k = lax.rem(i, nk)

        @pl.when(me - reach >= 0)
        def _():
            hop(elements, me, me - reach, k, -1).start()

        @pl.when(me + reach < n)
        def _():
            hop(elements, me, me + reach, k, 1).start()

        return carry

    lax.fori_loop(0, (n - 1) * nk, own_elements, 0)

    own_m.wait()
    own_occ.wait()
    weights = occ[pl.ds(k_minus_q[0], 1), :]
    band = lax.broadcasted_iota(jnp.int32, weights.shape, 1)
    acc[...] = jnp.zeros_like(acc)

    def w_block(g, h):
        if n_cycles % n == 0:
            cycles = n_cycles // n
            block = wbuf[pl.ds(g * cycles, cycles), :, :, lanes_of(h)]
        else:
            per_cycle = n * NB // g_slab
            start = lax.rem(g, per_cycle) * (g_slab // NB)
            block = wbuf[g // per_cycle, pl.ds(start, g_slab // NB), :, lanes_of(h)]
        return block.reshape(g_slab, g_slab)

    def bands(d, k):
        pair[...] = jnp.zeros_like(pair)

        def column_slab(h, carry):
            low = jnp.where(d > me, jnp.where(h == me, 0, me), jnp.where(d == me, jnp.where(h < me, me, 0), me))
            above = jnp.where(h > me, 0, me + 1)
            middle = jnp.where(h > me, me + 1, n)
            below = jnp.where(h == me, n, jnp.where(h > me, me + 1, 0))
            end = jnp.where(d > me, above, jnp.where(d == me, middle, below))

            @pl.when(low < end)
            def _():
                prod[...] = jnp.zeros_like(prod)

                def row_slab(g, inner):
                    left = mbuf[g, d, pl.ds(k * vg, vg)].reshape(vg * n_state, g_slab)
                    prod[...] += jnp.dot(left, w_block(g, h), preferred_element_type=jnp.float32)
                    return inner

                lax.fori_loop(low, end, row_slab, 0)
                for v in range(vg):
                    exact = prod[v * n_state : (v + 1) * n_state]
                    high_part = exact.astype(jnp.bfloat16)
                    low_part = (exact - high_part.astype(jnp.float32)).astype(jnp.bfloat16)
                    both = lax.dot_general(
                        jnp.concatenate([high_part, low_part], axis=0),
                        mbuf[h, d, k * vg + v],
                        (((1,), (1,)), ((), ())),
                        preferred_element_type=jnp.float32,
                    )
                    pair[v] += both[:n_state] + both[n_state:]

            return carry

        lax.fori_loop(0, n, column_slab, 0)
        for v in range(vg):
            here = band == d * v_per + k * vg + v
            weight = jnp.sum(jnp.where(here, weights, 0.0), axis=1, keepdims=True)
            acc[...] -= weight * pair[v]

    last_round = jnp.maximum(me, n - 1 - me)

    def round_of(distance, carry):
        low = me - distance
        high = me + distance

        def pass_w(i, inner):
            chunk = i // n
            h = lax.rem(i, n)

            @pl.when(jnp.logical_and(low >= 0, reaches_right(chunk, h, me)))
            def _():
                w_copy(low, chunk, h, 1).wait_recv()

                @pl.when(goes_right(chunk, h))
                def _():
                    w_copy(low, chunk, h, 1).start()

            @pl.when(jnp.logical_and(high < n, reaches_left(chunk, h, me)))
            def _():
                w_copy(high, chunk, h, -1).wait_recv()

                @pl.when(goes_left(chunk, h))
                def _():
                    w_copy(high, chunk, h, -1).start()

            return inner

        lax.fori_loop(0, nc * n, pass_w, 0)

        def pass_m(i, inner):
            reach = n - 1 - i // nk
            k = lax.rem(i, nk)

            @pl.when(jnp.logical_and(low >= 0, me + reach < n))
            def _():
                hop(None, low, me + reach, k, 1).wait_recv()
                hop(None, low, me + reach, k, 1).start()

            @pl.when(jnp.logical_and(high < n, me - reach >= 0))
            def _():
                hop(None, high, me - reach, k, -1).wait_recv()
                hop(None, high, me - reach, k, -1).start()

            @pl.when(jnp.logical_and(reach == 1, distance == last_round))
            def _():
                def others(d, most):
                    @pl.when(d != me)
                    def _():
                        bands(d, k)

                    return most

                lax.fori_loop(0, n, others, 0)

            return inner

        lax.fori_loop(0, (n - 1) * nk, pass_m, 0)
        return carry

    lax.fori_loop(1, n, round_of, 0)

    def own_bands(k, carry):
        for source in range(n):

            @pl.when(source != me)
            def _():
                hop(None, source, me, k, 1).wait_recv()

        bands(me, k)
        return carry

    lax.fori_loop(0, nk, own_bands, 0)

    def g_copy(offset):
        return pltpu.make_async_remote_copy(
            src_ref=parts.at[peer(offset)],
            dst_ref=ga_in.at[me],
            send_sem=gsend.at[offset - 1],
            recv_sem=grecv.at[offset - 1],
            device_id={"ga": peer(offset)},
            device_id_type=MESH,
        )

    parts[...] = jnp.zeros_like(parts)
    for j in range(n):
        parts[j, 0:rows, 0:n_state] = acc[j * rows : (j + 1) * rows, :]
    for offset in range(1, n):
        g_copy(offset).start()
    ga_in[me] = parts[me]
    for offset in range(1, n):
        g_copy(offset).wait_recv()
    total = ga_in[0]
    for j in range(1, n):
        total = total + ga_in[j]
    pb_in[my_pb] = total

    def p_copy(offset):
        return pltpu.make_async_remote_copy(
            src_ref=pb_in.at[my_pb],
            dst_ref=pb_in.at[my_pb],
            send_sem=psend.at[offset - 1],
            recv_sem=precv.at[offset - 1],
            device_id={"pb": pb_peer(offset)},
            device_id_type=MESH,
        )

    for offset in range(1, n_pb):
        p_copy(offset).start()
    for offset in range(1, n_pb):
        p_copy(offset).wait_recv()
    result = pb_in[0]
    for j in range(1, n_pb):
        result = result + pb_in[j]
    out[...] = result[0:rows, 0:n_state]

    for offset in range(1, n_pb):
        p_copy(offset).wait_send()
    for offset in range(1, n):
        g_copy(offset).wait_send()

    def sent_elements(i, carry):
        source = i // (n * nk)
        target = lax.rem(i // nk, n)
        k = lax.rem(i, nk)

        @pl.when(jnp.logical_and(source == me, target != me))
        def _():
            hop(elements, source, target, k, 1).wait_send()

        passed = jnp.logical_or(
            jnp.logical_and(source < me, target > me), jnp.logical_and(source > me, target < me)
        )

        @pl.when(passed)
        def _():
            hop(None, source, target, k, 1).wait_send()

        return carry

    lax.fori_loop(0, n * n * nk, sent_elements, 0)

    def sent_pieces(i, carry):
        source = i // (nc * n)
        chunk = lax.rem(i // n, nc)
        h = lax.rem(i, n)

        @pl.when(jnp.logical_and(source >= me, goes_left(chunk, h)))
        def _():
            w_copy(source, chunk, h, -1).wait_send()

        @pl.when(jnp.logical_and(source <= me, goes_right(chunk, h)))
        def _():
            w_copy(source, chunk, h, 1).wait_send()

        return carry

    lax.fori_loop(0, n * nc * n, sent_pieces, 0)


def on_device(n, n_pb, elements, screened, counts, k_minus_q, occupation):
    _, n_band, n_state, g_slab = elements.shape
    g_total = screened.shape[2]
    v_per = n_band // n
    n_cycles = g_slab // NB
    vg = 4 if v_per % 4 == 0 else 1
    nc = min(4, n_cycles)
    wc = n_cycles // nc
    nk = v_per // vg
    rows = n_state // n
    padded = (rows + 7) // 8 * 8
    lanes = (n_state + 127) // 128 * 128
    any_spec = pl.BlockSpec(memory_space=pl.ANY)
    smem = pl.BlockSpec(memory_space=pltpu.SMEM)
    vmem = pl.BlockSpec(memory_space=pltpu.VMEM)
    dma = pltpu.SemaphoreType.DMA
    return pl.pallas_call(
        functools.partial(kernel, n, n_pb, vg, wc),
        out_shape=jax.ShapeDtypeStruct((rows, n_state), jnp.float32),
        in_specs=[any_spec, any_spec, smem, smem, any_spec],
        out_specs=vmem,
        scratch_shapes=[
            pltpu.VMEM((n, n, v_per, n_state, g_slab), jnp.bfloat16),
            pltpu.VMEM((n_cycles, n, NB, g_total), jnp.bfloat16),
            pltpu.VMEM((n_cycles, NB, g_total), jnp.bfloat16),
            pltpu.VMEM(occupation.shape, jnp.float32),
            pltpu.VMEM((vg * n_state, g_slab), jnp.float32),
            pltpu.VMEM((vg, n_state, n_state), jnp.float32),
            pltpu.VMEM((n_state, n_state), jnp.float32),
            pltpu.VMEM((n, padded, lanes), jnp.float32),
            pltpu.VMEM((n, padded, lanes), jnp.float32),
            pltpu.VMEM((n_pb, padded, lanes), jnp.float32),
            dma((3,)),
            dma((2, n, nc * n)),
            dma((n, nc * n)),
            dma((n, n, nk)),
            dma((n, n, nk)),
            dma((n - 1,)),
            dma((n - 1,)),
            dma((n_pb - 1,)),
            dma((n_pb - 1,)),
        ],
        compiler_params=pltpu.CompilerParams(
            collective_id=0, has_side_effects=True, vmem_limit_bytes=56 * 1024 * 1024
        ),
        cost_estimate=pl.CostEstimate(
            flops=2 * v_per * n_state * g_total * (g_total + n_state),
            bytes_accessed=16 * 1024 * 1024,
            transcendentals=0,
        ),
    )(
        elements.reshape(n, v_per, n_state, g_slab),
        screened.reshape(n_cycles, NB, g_total),
        counts,
        k_minus_q,
        occupation,
    )


def solution(mesh):
    return jax.shard_map(
        functools.partial(on_device, mesh.shape["ga"], mesh.shape["pb"]),
        mesh=mesh,
        in_specs=(P("pb", None, None, "ga"), P("pb", "ga", None), P("pb"), P("pb"), P()),
        out_specs=P("ga", None),
        check_vma=False,
    )
```

```python
import functools

import jax
import jax.numpy as jnp
from jax import lax
from jax.experimental import pallas as pl
from jax.experimental.pallas import tpu as pltpu
from jax.sharding import PartitionSpec as P

NB = 32
MESH = pl.DeviceIdType.MESH


def kernel(
    n, n_pb, vg, wc,
    elements, screened, counts, k_minus_q, occupation, out,
    mbuf, wbuf, wown, occ, weights, prod, pair, acc, parts, ga_in, pb_in,
    local_sem, wsend, wrecv, msend, mrecv, gsend, grecv, psend, precv,
):
    me = lax.axis_index("ga")
    my_pb = lax.axis_index("pb")
    _, v_per, n_state, g_slab = elements.shape
    n_cycles, _, g_total = screened.shape
    rows = n_state // n
    nk = v_per // vg
    nc = n_cycles // wc
    group = 2 if nk % 2 == 0 else 1

    def peer(offset):
        return lax.rem(me + offset, n)

    def pb_peer(offset):
        return lax.rem(my_pb + offset, n_pb)

    own_w = pltpu.make_async_copy(screened, wown, local_sem.at[0])
    own_m = pltpu.make_async_copy(elements, mbuf.at[me], local_sem.at[1])
    own_occ = pltpu.make_async_copy(occupation, occ, local_sem.at[2])
    own_w.start()
    own_m.start()
    own_occ.start()

    barrier = pltpu.get_barrier_semaphore()
    for offset in range(1, n):
        pl.semaphore_signal(barrier, inc=1, device_id={"ga": peer(offset)}, device_id_type=MESH)
    for offset in range(1, n_pb):
        pl.semaphore_signal(barrier, inc=1, device_id={"pb": pb_peer(offset)}, device_id_type=MESH)
    pl.semaphore_wait(barrier, n - 1 + n_pb - 1)

    def hop(src, source, target, k, step):
        here = (source, target, pl.ds(k * vg, vg))
        return pltpu.make_async_remote_copy(
            src_ref=mbuf.at[here] if src is None else src.at[target, pl.ds(k * vg, vg)],
            dst_ref=mbuf.at[here],
            send_sem=msend.at[source, target, k],
            recv_sem=mrecv.at[source, target, k],
            device_id={"ga": lax.rem(me + step + n, n)},
            device_id_type=MESH,
        )

    def lanes_of(h):
        return pl.ds(pl.multiple_of(h * g_slab, g_slab), g_slab)

    def first_slab(chunk):
        return chunk * wc * n * NB // g_slab

    def last_slab(chunk):
        return ((chunk + 1) * wc * n * NB - 1) // g_slab

    def reaches_left(chunk, h, device):
        return jnp.logical_or(first_slab(chunk) <= device, h <= device)

    def reaches_right(chunk, h, device):
        return jnp.logical_or(last_slab(chunk) >= device, h >= device)

    def w_copy(source, chunk, h, step):
        slot = source if step < 0 else jnp.where(source == me, n, source)
        piece = chunk * n + h
        here = (pl.ds(chunk * wc, wc), source, slice(None), lanes_of(h))
        return pltpu.make_async_remote_copy(
            src_ref=wbuf.at[here],
            dst_ref=wbuf.at[here],
            send_sem=wsend.at[slot, piece],
            recv_sem=wrecv.at[source, piece],
            device_id={"ga": lax.rem(me + step + n, n)},
            device_id_type=MESH,
        )

    def goes_left(chunk, h):
        return jnp.logical_and(me > 0, reaches_left(chunk, h, me - 1))

    def goes_right(chunk, h):
        return jnp.logical_and(me < n - 1, reaches_right(chunk, h, me + 1))

    def send_elements(reach, k):
        @pl.when(me - reach >= 0)
        def _():
            hop(elements, me, me - reach, k, -1).start()

        @pl.when(me + reach < n)
        def _():
            hop(elements, me, me + reach, k, 1).start()

    def first_elements(i, carry):
        send_elements(n - 1 - i, 0)
        return carry

    def more_elements(i, carry):
        send_elements(n - 1 - i // (nk - 1), 1 + lax.rem(i, nk - 1))
        return carry

    lax.fori_loop(0, n - 1, first_elements, 0)
    own_w.wait()
    count = counts[0]
    column = lax.broadcasted_iota(jnp.int32, (NB, g_total), 1)
    row = lax.broadcasted_iota(jnp.int32, (NB, g_total), 0)

    for chunk in range(nc):

        def mask_block(c, carry):
            g = row + (c * n + me) * NB
            inside = jnp.logical_and(g < count, column < count)
            block = wown[c].astype(jnp.float32)
            wbuf[c, me] = jnp.where(inside, block, 0.0).astype(jnp.bfloat16)
            return carry

        lax.fori_loop(chunk * wc, (chunk + 1) * wc, mask_block, 0)

        def send_own(h, carry):
            @pl.when(goes_left(chunk, h))
            def _():
                w_copy(me, chunk, h, -1).start()

            @pl.when(goes_right(chunk, h))
            def _():
                w_copy(me, chunk, h, 1).start()

            return carry

        lax.fori_loop(0, n, send_own, 0)

    lax.fori_loop(0, (n - 1) * (nk - 1), more_elements, 0)

    own_m.wait()
    own_occ.wait()
    k_points = lax.broadcasted_iota(jnp.int32, occ.shape, 1)
    chosen = jnp.where(k_points == k_minus_q[0], occ[...], 0.0)
    weights[...] = jnp.broadcast_to(jnp.sum(chosen, axis=1, keepdims=True), weights.shape)
    acc[...] = jnp.zeros_like(acc)

    def w_block(g, h):
        if n_cycles % n == 0:
            cycles = n_cycles // n
            block = wbuf[pl.ds(g * cycles, cycles), :, :, lanes_of(h)]
        else:
            per_cycle = n * NB // g_slab
            start = lax.rem(g, per_cycle) * (g_slab // NB)
            block = wbuf[g // per_cycle, pl.ds(start, g_slab // NB), :, lanes_of(h)]
        return block.reshape(g_slab, g_slab)

    def bands(d, first, size):
        pair[...] = jnp.zeros_like(pair)

        def column_slab(h, carry):
            low = jnp.where(d > me, jnp.where(h == me, 0, me), jnp.where(d == me, jnp.where(h < me, me, 0), me))
            above = jnp.where(h > me, 0, me + 1)
            middle = jnp.where(h > me, me + 1, n)
            below = jnp.where(h == me, n, jnp.where(h > me, me + 1, 0))
            end = jnp.where(d > me, above, jnp.where(d == me, middle, below))

            @pl.when(low < end)
            def _():
                prod[0 : size * n_state] = jnp.zeros((size * n_state, g_slab), jnp.float32)

                def row_slab(g, inner):
                    left = mbuf[g, d, pl.ds(first, size)].reshape(size * n_state, g_slab)
                    prod[0 : size * n_state] += jnp.dot(
                        left, w_block(g, h), preferred_element_type=jnp.float32
                    )
                    return inner

                lax.fori_loop(low, end, row_slab, 0)
                for v in range(size):
                    exact = prod[v * n_state : (v + 1) * n_state]
                    high_part = exact.astype(jnp.bfloat16)
                    low_part = (exact - high_part.astype(jnp.float32)).astype(jnp.bfloat16)
                    both = lax.dot_general(
                        jnp.concatenate([high_part, low_part], axis=0),
                        mbuf[h, d, first + v],
                        (((1,), (1,)), ((), ())),
                        preferred_element_type=jnp.float32,
                    )
                    pair[v] += both[:n_state] + both[n_state:]

            return carry

        lax.fori_loop(0, n, column_slab, 0)
        for v in range(size):
            weight = weights[pl.ds(d * v_per + first + v, 1), 0:n_state]
            acc[...] -= weight * pair[v]

    last_round = jnp.maximum(me, n - 1 - me)

    def round_of(distance, carry):
        low = me - distance
        high = me + distance

        def pass_w(i, inner):
            chunk = i // n
            h = lax.rem(i, n)

            @pl.when(jnp.logical_and(low >= 0, reaches_right(chunk, h, me)))
            def _():
                w_copy(low, chunk, h, 1).wait_recv()

                @pl.when(goes_right(chunk, h))
                def _():
                    w_copy(low, chunk, h, 1).start()

            @pl.when(jnp.logical_and(high < n, reaches_left(chunk, h, me)))
            def _():
                w_copy(high, chunk, h, -1).wait_recv()

                @pl.when(goes_left(chunk, h))
                def _():
                    w_copy(high, chunk, h, -1).start()

            return inner

        lax.fori_loop(0, nc * n, pass_w, 0)

        def pass_m(i, inner):
            reach = n - 1 - i // nk
            k = lax.rem(i, nk)

            @pl.when(jnp.logical_and(low >= 0, me + reach < n))
            def _():
                hop(None, low, me + reach, k, 1).wait_recv()
                hop(None, low, me + reach, k, 1).start()

            @pl.when(jnp.logical_and(high < n, me - reach >= 0))
            def _():
                hop(None, high, me - reach, k, -1).wait_recv()
                hop(None, high, me - reach, k, -1).start()

            group_ends = lax.rem(k, group) == group - 1

            @pl.when(jnp.logical_and(jnp.logical_and(reach == 1, group_ends), distance == last_round))
            def _():
                def others(d, most):
                    @pl.when(d != me)
                    def _():
                        bands(d, (k - (group - 1)) * vg, group * vg)

                    return most

                lax.fori_loop(0, n, others, 0)

            return inner

        lax.fori_loop(0, (n - 1) * nk, pass_m, 0)
        return carry

    lax.fori_loop(1, n, round_of, 0)

    def arrived(k):
        for source in range(n):

            @pl.when(source != me)
            def _():
                hop(None, source, me, k, 1).wait_recv()

    def own_group(i, carry):
        for j in range(group):
            arrived(i * group + j)
        bands(me, i * group * vg, group * vg)
        return carry

    lax.fori_loop(0, nk // group - 1, own_group, 0)
    for k in range(nk - group, nk):
        arrived(k)
        bands(me, k * vg, vg)

    def g_copy(offset):
        return pltpu.make_async_remote_copy(
            src_ref=parts.at[peer(offset)],
            dst_ref=ga_in.at[me],
            send_sem=gsend.at[offset - 1],
            recv_sem=grecv.at[offset - 1],
            device_id={"ga": peer(offset)},
            device_id_type=MESH,
        )

    parts[...] = jnp.zeros_like(parts)
    for j in range(n):
        parts[j, 0:rows, 0:n_state] = acc[j * rows : (j + 1) * rows, :]
    for offset in range(1, n):
        g_copy(offset).start()
    ga_in[me] = parts[me]
    for offset in range(1, n):
        g_copy(offset).wait_recv()
    total = ga_in[0]
    for j in range(1, n):
        total = total + ga_in[j]
    pb_in[my_pb] = total

    def p_copy(offset):
        return pltpu.make_async_remote_copy(
            src_ref=pb_in.at[my_pb],
            dst_ref=pb_in.at[my_pb],
            send_sem=psend.at[offset - 1],
            recv_sem=precv.at[offset - 1],
            device_id={"pb": pb_peer(offset)},
            device_id_type=MESH,
        )

    for offset in range(1, n_pb):
        p_copy(offset).start()
    for offset in range(1, n_pb):
        p_copy(offset).wait_recv()
    result = pb_in[0]
    for j in range(1, n_pb):
        result = result + pb_in[j]
    out[...] = result[0:rows, 0:n_state]

    for offset in range(1, n_pb):
        p_copy(offset).wait_send()
    for offset in range(1, n):
        g_copy(offset).wait_send()

    def sent_elements(i, carry):
        source = i // (n * nk)
        target = lax.rem(i // nk, n)
        k = lax.rem(i, nk)

        @pl.when(jnp.logical_and(source == me, target != me))
        def _():
            hop(elements, source, target, k, 1).wait_send()

        passed = jnp.logical_or(
            jnp.logical_and(source < me, target > me), jnp.logical_and(source > me, target < me)
        )

        @pl.when(passed)
        def _():
            hop(None, source, target, k, 1).wait_send()

        return carry

    lax.fori_loop(0, n * n * nk, sent_elements, 0)

    def sent_pieces(i, carry):
        source = i // (nc * n)
        chunk = lax.rem(i // n, nc)
        h = lax.rem(i, n)

        @pl.when(jnp.logical_and(source >= me, goes_left(chunk, h)))
        def _():
            w_copy(source, chunk, h, -1).wait_send()

        @pl.when(jnp.logical_and(source <= me, goes_right(chunk, h)))
        def _():
            w_copy(source, chunk, h, 1).wait_send()

        return carry

    lax.fori_loop(0, n * nc * n, sent_pieces, 0)


def on_device(n, n_pb, elements, screened, counts, k_minus_q, occupation):
    _, n_band, n_state, g_slab = elements.shape
    g_total = screened.shape[2]
    v_per = n_band // n
    n_cycles = g_slab // NB
    vg = 2 if v_per % 4 == 0 else 1
    nc = min(4, n_cycles)
    wc = n_cycles // nc
    nk = v_per // vg
    group = 2 if nk % 2 == 0 else 1
    rows = n_state // n
    padded = (rows + 7) // 8 * 8
    lanes = (n_state + 127) // 128 * 128
    any_spec = pl.BlockSpec(memory_space=pl.ANY)
    smem = pl.BlockSpec(memory_space=pltpu.SMEM)
    vmem = pl.BlockSpec(memory_space=pltpu.VMEM)
    dma = pltpu.SemaphoreType.DMA
    return pl.pallas_call(
        functools.partial(kernel, n, n_pb, vg, wc),
        out_shape=jax.ShapeDtypeStruct((rows, n_state), jnp.float32),
        in_specs=[any_spec, any_spec, smem, smem, any_spec],
        out_specs=vmem,
        scratch_shapes=[
            pltpu.VMEM((n, n, v_per, n_state, g_slab), jnp.bfloat16),
            pltpu.VMEM((n_cycles, n, NB, g_total), jnp.bfloat16),
            pltpu.VMEM((n_cycles, NB, g_total), jnp.bfloat16),
            pltpu.VMEM(occupation.shape[::-1], jnp.float32),
            pltpu.VMEM((n_band, lanes), jnp.float32),
            pltpu.VMEM((group * vg * n_state, g_slab), jnp.float32),
            pltpu.VMEM((group * vg, n_state, n_state), jnp.float32),
            pltpu.VMEM((n_state, n_state), jnp.float32),
            pltpu.VMEM((n, padded, lanes), jnp.float32),
            pltpu.VMEM((n, padded, lanes), jnp.float32),
            pltpu.VMEM((n_pb, padded, lanes), jnp.float32),
            dma((3,)),
            dma((n + 1, nc * n)),
            dma((n, nc * n)),
            dma((n, n, nk)),
            dma((n, n, nk)),
            dma((n - 1,)),
            dma((n - 1,)),
            dma((n_pb - 1,)),
            dma((n_pb - 1,)),
        ],
        compiler_params=pltpu.CompilerParams(
            collective_id=0, has_side_effects=True, vmem_limit_bytes=56 * 1024 * 1024
        ),
        cost_estimate=pl.CostEstimate(
            flops=2 * v_per * n_state * g_total * (g_total + n_state),
            bytes_accessed=16 * 1024 * 1024,
            transcendentals=0,
        ),
    )(
        elements.reshape(n, v_per, n_state, g_slab),
        screened.reshape(n_cycles, NB, g_total),
        counts,
        k_minus_q,
        occupation.T,
    )


def solution(mesh):
    return jax.shard_map(
        functools.partial(on_device, mesh.shape["ga"], mesh.shape["pb"]),
        mesh=mesh,
        in_specs=(P("pb", None, None, "ga"), P("pb", "ga", None), P("pb"), P("pb"), P()),
        out_specs=P("ga", None),
        check_vma=False,
    )
```

```python
import functools

import jax
import jax.numpy as jnp
from jax import lax
from jax.experimental import pallas as pl
from jax.experimental.pallas import tpu as pltpu
from jax.sharding import PartitionSpec as P

NB = 32
MESH = pl.DeviceIdType.MESH


def kernel(
    n, n_pb, vg, wc,
    elements, screened, counts, k_minus_q, occupation, out,
    mbuf, wbuf, wown, occ, weights, prod, pair, acc, parts, ga_in, pb_in,
    local_sem, wsend, wrecv, msend, mrecv, gsend, grecv, psend, precv,
):
    me = lax.axis_index("ga")
    my_pb = lax.axis_index("pb")
    _, v_per, n_state, g_slab = elements.shape
    n_cycles, _, g_total = screened.shape
    rows = n_state // n
    nk = v_per // vg
    nc = n_cycles // wc
    group = 2 if nk % 2 == 0 else 1

    def peer(offset):
        return lax.rem(me + offset, n)

    def pb_peer(offset):
        return lax.rem(my_pb + offset, n_pb)

    own_w = pltpu.make_async_copy(screened, wown, local_sem.at[0])
    own_m = pltpu.make_async_copy(elements, mbuf.at[me], local_sem.at[1])
    own_occ = pltpu.make_async_copy(occupation, occ, local_sem.at[2])
    own_w.start()
    own_m.start()
    own_occ.start()

    barrier = pltpu.get_barrier_semaphore()
    for offset in range(1, n):
        pl.semaphore_signal(barrier, inc=1, device_id={"ga": peer(offset)}, device_id_type=MESH)
    for offset in range(1, n_pb):
        pl.semaphore_signal(barrier, inc=1, device_id={"pb": pb_peer(offset)}, device_id_type=MESH)
    pl.semaphore_wait(barrier, n - 1 + n_pb - 1)

    def hop(src, source, target, k, step):
        here = (source, target, pl.ds(k * vg, vg))
        return pltpu.make_async_remote_copy(
            src_ref=mbuf.at[here] if src is None else src.at[target, pl.ds(k * vg, vg)],
            dst_ref=mbuf.at[here],
            send_sem=msend.at[source, target, k],
            recv_sem=mrecv.at[source, target, k],
            device_id={"ga": lax.rem(me + step + n, n)},
            device_id_type=MESH,
        )

    def lanes_of(h):
        return pl.ds(pl.multiple_of(h * g_slab, g_slab), g_slab)

    def first_slab(chunk):
        return chunk * wc * n * NB // g_slab

    def last_slab(chunk):
        return ((chunk + 1) * wc * n * NB - 1) // g_slab

    def reaches_left(chunk, h, device):
        return jnp.logical_or(first_slab(chunk) <= device, h <= device)

    def reaches_right(chunk, h, device):
        return jnp.logical_or(last_slab(chunk) >= device, h >= device)

    def w_copy(source, chunk, h, step):
        slot = source if step < 0 else jnp.where(source == me, n, source)
        piece = chunk * n + h
        here = (pl.ds(chunk * wc, wc), source, slice(None), lanes_of(h))
        return pltpu.make_async_remote_copy(
            src_ref=wbuf.at[here],
            dst_ref=wbuf.at[here],
            send_sem=wsend.at[slot, piece],
            recv_sem=wrecv.at[source, piece],
            device_id={"ga": lax.rem(me + step + n, n)},
            device_id_type=MESH,
        )

    def goes_left(chunk, h):
        return jnp.logical_and(me > 0, reaches_left(chunk, h, me - 1))

    def goes_right(chunk, h):
        return jnp.logical_and(me < n - 1, reaches_right(chunk, h, me + 1))

    def send_elements(reach, k):
        @pl.when(me - reach >= 0)
        def _():
            hop(elements, me, me - reach, k, -1).start()

        @pl.when(me + reach < n)
        def _():
            hop(elements, me, me + reach, k, 1).start()

    def first_elements(i, carry):
        send_elements(n - 1 - i, 0)
        return carry

    def more_elements(i, carry):
        send_elements(n - 1 - i // (nk - 1), 1 + lax.rem(i, nk - 1))
        return carry

    lax.fori_loop(0, n - 1, first_elements, 0)
    own_w.wait()
    count = counts[0]
    column = lax.broadcasted_iota(jnp.int32, (NB, g_total), 1)
    row = lax.broadcasted_iota(jnp.int32, (NB, g_total), 0)

    for chunk in range(nc):

        def mask_block(c, carry):
            g = row + (c * n + me) * NB
            inside = jnp.logical_and(g < count, column < count)
            block = wown[c].astype(jnp.float32)
            wbuf[c, me] = jnp.where(inside, block, 0.0).astype(jnp.bfloat16)
            return carry

        lax.fori_loop(chunk * wc, (chunk + 1) * wc, mask_block, 0)

        def send_own(h, carry):
            @pl.when(goes_left(chunk, h))
            def _():
                w_copy(me, chunk, h, -1).start()

            @pl.when(goes_right(chunk, h))
            def _():
                w_copy(me, chunk, h, 1).start()

            return carry

        lax.fori_loop(0, n, send_own, 0)

    own_m.wait()
    own_occ.wait()
    k_points = lax.broadcasted_iota(jnp.int32, occ.shape, 1)
    chosen = jnp.where(k_points == k_minus_q[0], occ[...], 0.0)
    weights[...] = jnp.broadcast_to(jnp.sum(chosen, axis=1, keepdims=True), weights.shape)
    acc[...] = jnp.zeros_like(acc)

    def w_block(g, h):
        if n_cycles % n == 0:
            cycles = n_cycles // n
            block = wbuf[pl.ds(g * cycles, cycles), :, :, lanes_of(h)]
        else:
            per_cycle = n * NB // g_slab
            start = lax.rem(g, per_cycle) * (g_slab // NB)
            block = wbuf[g // per_cycle, pl.ds(start, g_slab // NB), :, lanes_of(h)]
        return block.reshape(g_slab, g_slab)

    far = jnp.where(2 * me < n, n - 1, 0)

    def bands(d, first, size, part=None):
        pair[...] = jnp.zeros_like(pair)

        def column_slab(h, carry):
            low = jnp.where(d > me, jnp.where(h == me, 0, me), jnp.where(d == me, jnp.where(h < me, me, 0), me))
            above = jnp.where(h > me, 0, me + 1)
            middle = jnp.where(h > me, me + 1, n)
            below = jnp.where(h == me, n, jnp.where(h > me, me + 1, 0))
            end = jnp.where(d > me, above, jnp.where(d == me, middle, below))
            if part == "near":
                low = jnp.where(far == 0, jnp.maximum(low, 1), low)
                end = jnp.where(h == far, 0, jnp.where(far == 0, end, jnp.minimum(end, n - 1)))
            if part == "far":
                has_far = jnp.logical_and(low <= far, far < end)
                low = jnp.where(h == far, low, far)
                end = jnp.where(h == far, end, jnp.where(has_far, far + 1, 0))

            @pl.when(low < end)
            def _():
                prod[0 : size * n_state] = jnp.zeros((size * n_state, g_slab), jnp.float32)

                def row_slab(g, inner):
                    left = mbuf[g, d, pl.ds(first, size)].reshape(size * n_state, g_slab)
                    prod[0 : size * n_state] += jnp.dot(
                        left, w_block(g, h), preferred_element_type=jnp.float32
                    )
                    return inner

                lax.fori_loop(low, end, row_slab, 0)
                for v in range(size):
                    exact = prod[v * n_state : (v + 1) * n_state]
                    high_part = exact.astype(jnp.bfloat16)
                    low_part = (exact - high_part.astype(jnp.float32)).astype(jnp.bfloat16)
                    both = lax.dot_general(
                        jnp.concatenate([high_part, low_part], axis=0),
                        mbuf[h, d, first + v],
                        (((1,), (1,)), ((), ())),
                        preferred_element_type=jnp.float32,
                    )
                    pair[v] += both[:n_state] + both[n_state:]

            return carry

        lax.fori_loop(0, n, column_slab, 0)
        for v in range(size):
            weight = weights[pl.ds(d * v_per + first + v, 1), 0:n_state]
            acc[...] -= weight * pair[v]

    def w_round(distance, carry):
        low = me - distance
        high = me + distance

        def pass_w(i, inner):
            chunk = i // n
            h = lax.rem(i, n)

            @pl.when(jnp.logical_and(low >= 0, reaches_right(chunk, h, me)))
            def _():
                w_copy(low, chunk, h, 1).wait_recv()

                @pl.when(goes_right(chunk, h))
                def _():
                    w_copy(low, chunk, h, 1).start()

            @pl.when(jnp.logical_and(high < n, reaches_left(chunk, h, me)))
            def _():
                w_copy(high, chunk, h, -1).wait_recv()

                @pl.when(goes_left(chunk, h))
                def _():
                    w_copy(high, chunk, h, -1).start()

            return inner

        lax.fori_loop(0, nc * n, pass_w, 0)
        return carry

    total_more = (n - 1) * (nk - 1)

    def w_and_elements(distance, carry):
        share = (total_more + n - 2) // (n - 1)
        start = (distance - 1) * share
        lax.fori_loop(start, jnp.minimum(start + share, total_more), more_elements, 0)
        return w_round(distance, carry)

    lax.fori_loop(1, n, w_and_elements, 0)

    def round_of(distance, carry):
        low = me - distance
        high = me + distance

        def pass_m(i, inner):
            reach = n - 1 - i // nk
            k = lax.rem(i, nk)

            @pl.when(jnp.logical_and(low >= 0, me + reach < n))
            def _():
                hop(None, low, me + reach, k, 1).wait_recv()
                hop(None, low, me + reach, k, 1).start()

            @pl.when(jnp.logical_and(high < n, me - reach >= 0))
            def _():
                hop(None, high, me - reach, k, -1).wait_recv()
                hop(None, high, me - reach, k, -1).start()

            group_ends = lax.rem(k, group) == group - 1
            first = (k - (group - 1)) * vg
            to_right = jnp.logical_and(me + reach < n, distance == jnp.maximum(me, 1))
            to_left = jnp.logical_and(me - reach >= 0, distance == jnp.maximum(n - 1 - me, 1))

            def side(j, most):
                d = jnp.where(j == 0, me + reach, me - reach)
                wanted = jnp.where(j == 0, to_right, to_left)

                @pl.when(jnp.logical_and(group_ends, wanted))
                def _():
                    bands(d, first, group * vg)

                return most

            lax.fori_loop(0, 2, side, 0)
            return inner

        lax.fori_loop(0, (n - 1) * nk, pass_m, 0)
        return carry

    lax.fori_loop(1, n, round_of, 0)

    def arrived(k, is_far):
        for source in range(n):

            @pl.when(jnp.logical_and(source != me, (far == source) == is_far))
            def _():
                hop(None, source, me, k, 1).wait_recv()

    def near_group(i, carry):
        for j in range(group):
            arrived(i * group + j, False)
        bands(me, i * group * vg, group * vg, "near")
        return carry

    lax.fori_loop(0, nk // group, near_group, 0)

    def far_group(k, carry):
        arrived(k, True)
        bands(me, k * vg, vg, "far")
        return carry

    lax.fori_loop(0, nk, far_group, 0)

    def g_copy(offset):
        return pltpu.make_async_remote_copy(
            src_ref=parts.at[peer(offset)],
            dst_ref=ga_in.at[me],
            send_sem=gsend.at[offset - 1],
            recv_sem=grecv.at[offset - 1],
            device_id={"ga": peer(offset)},
            device_id_type=MESH,
        )

    parts[...] = jnp.zeros_like(parts)
    for j in range(n):
        parts[j, 0:rows, 0:n_state] = acc[j * rows : (j + 1) * rows, :]
    for offset in range(1, n):
        g_copy(offset).start()
    ga_in[me] = parts[me]
    for offset in range(1, n):
        g_copy(offset).wait_recv()
    total = ga_in[0]
    for j in range(1, n):
        total = total + ga_in[j]
    pb_in[my_pb] = total

    def p_copy(offset):
        return pltpu.make_async_remote_copy(
            src_ref=pb_in.at[my_pb],
            dst_ref=pb_in.at[my_pb],
            send_sem=psend.at[offset - 1],
            recv_sem=precv.at[offset - 1],
            device_id={"pb": pb_peer(offset)},
            device_id_type=MESH,
        )

    for offset in range(1, n_pb):
        p_copy(offset).start()
    for offset in range(1, n_pb):
        p_copy(offset).wait_recv()
    result = pb_in[0]
    for j in range(1, n_pb):
        result = result + pb_in[j]
    out[...] = result[0:rows, 0:n_state]

    for offset in range(1, n_pb):
        p_copy(offset).wait_send()
    for offset in range(1, n):
        g_copy(offset).wait_send()

    def sent_elements(i, carry):
        source = i // (n * nk)
        target = lax.rem(i // nk, n)
        k = lax.rem(i, nk)

        @pl.when(jnp.logical_and(source == me, target != me))
        def _():
            hop(elements, source, target, k, 1).wait_send()

        passed = jnp.logical_or(
            jnp.logical_and(source < me, target > me), jnp.logical_and(source > me, target < me)
        )

        @pl.when(passed)
        def _():
            hop(None, source, target, k, 1).wait_send()

        return carry

    lax.fori_loop(0, n * n * nk, sent_elements, 0)

    def sent_pieces(i, carry):
        source = i // (nc * n)
        chunk = lax.rem(i // n, nc)
        h = lax.rem(i, n)

        @pl.when(jnp.logical_and(source >= me, goes_left(chunk, h)))
        def _():
            w_copy(source, chunk, h, -1).wait_send()

        @pl.when(jnp.logical_and(source <= me, goes_right(chunk, h)))
        def _():
            w_copy(source, chunk, h, 1).wait_send()

        return carry

    lax.fori_loop(0, n * nc * n, sent_pieces, 0)


def on_device(n, n_pb, elements, screened, counts, k_minus_q, occupation):
    _, n_band, n_state, g_slab = elements.shape
    g_total = screened.shape[2]
    v_per = n_band // n
    n_cycles = g_slab // NB
    vg = 2 if v_per % 4 == 0 else 1
    nc = min(4, n_cycles)
    wc = n_cycles // nc
    nk = v_per // vg
    group = 2 if nk % 2 == 0 else 1
    rows = n_state // n
    padded = (rows + 7) // 8 * 8
    lanes = (n_state + 127) // 128 * 128
    any_spec = pl.BlockSpec(memory_space=pl.ANY)
    smem = pl.BlockSpec(memory_space=pltpu.SMEM)
    vmem = pl.BlockSpec(memory_space=pltpu.VMEM)
    dma = pltpu.SemaphoreType.DMA
    return pl.pallas_call(
        functools.partial(kernel, n, n_pb, vg, wc),
        out_shape=jax.ShapeDtypeStruct((rows, n_state), jnp.float32),
        in_specs=[any_spec, any_spec, smem, smem, any_spec],
        out_specs=vmem,
        scratch_shapes=[
            pltpu.VMEM((n, n, v_per, n_state, g_slab), jnp.bfloat16),
            pltpu.VMEM((n_cycles, n, NB, g_total), jnp.bfloat16),
            pltpu.VMEM((n_cycles, NB, g_total), jnp.bfloat16),
            pltpu.VMEM(occupation.shape[::-1], jnp.float32),
            pltpu.VMEM((n_band, lanes), jnp.float32),
            pltpu.VMEM((group * vg * n_state, g_slab), jnp.float32),
            pltpu.VMEM((group * vg, n_state, n_state), jnp.float32),
            pltpu.VMEM((n_state, n_state), jnp.float32),
            pltpu.VMEM((n, padded, lanes), jnp.float32),
            pltpu.VMEM((n, padded, lanes), jnp.float32),
            pltpu.VMEM((n_pb, padded, lanes), jnp.float32),
            dma((3,)),
            dma((n + 1, nc * n)),
            dma((n, nc * n)),
            dma((n, n, nk)),
            dma((n, n, nk)),
            dma((n - 1,)),
            dma((n - 1,)),
            dma((n_pb - 1,)),
            dma((n_pb - 1,)),
        ],
        compiler_params=pltpu.CompilerParams(
            collective_id=0, has_side_effects=True, vmem_limit_bytes=56 * 1024 * 1024
        ),
        cost_estimate=pl.CostEstimate(
            flops=2 * v_per * n_state * g_total * (g_total + n_state),
            bytes_accessed=16 * 1024 * 1024,
            transcendentals=0,
        ),
    )(
        elements.reshape(n, v_per, n_state, g_slab),
        screened.reshape(n_cycles, NB, g_total),
        counts,
        k_minus_q,
        occupation.T,
    )


def solution(mesh):
    return jax.shard_map(
        functools.partial(on_device, mesh.shape["ga"], mesh.shape["pb"]),
        mesh=mesh,
        in_specs=(P("pb", None, None, "ga"), P("pb", "ga", None), P("pb"), P("pb"), P()),
        out_specs=P("ga", None),
        check_vma=False,
    )
```

```python
import functools

import jax
import jax.numpy as jnp
from jax import lax
from jax.experimental import pallas as pl
from jax.experimental.pallas import tpu as pltpu
from jax.sharding import PartitionSpec as P

NB = 32
MESH = pl.DeviceIdType.MESH


def kernel(
    n, n_pb, vg, wc,
    elements, screened, counts, k_minus_q, occupation, out,
    mbuf, wbuf, wown, occ, weights, prod, pair, acc, parts, ga_in, pb_in,
    local_sem, wsend, wrecv, msend, mrecv, gsend, grecv, psend, precv,
):
    me = lax.axis_index("ga")
    my_pb = lax.axis_index("pb")
    _, v_per, n_state, g_slab = elements.shape
    n_cycles, _, g_total = screened.shape
    rows = n_state // n
    nk = v_per // vg
    span = 2 * nk
    half = n // 2
    base = lax.rem(my_pb, 2) * half
    nc = n_cycles // wc
    group = 2 if nk % 2 == 0 else 1

    def peer(offset):
        return lax.rem(me + offset, n)

    def pb_peer(offset):
        return lax.rem(my_pb + offset, n_pb)

    own_w = pltpu.make_async_copy(screened, wown, local_sem.at[0])
    own_m = pltpu.make_async_copy(elements, mbuf.at[me], local_sem.at[1])
    own_occ = pltpu.make_async_copy(occupation, occ, local_sem.at[2])
    own_w.start()
    own_m.start()
    own_occ.start()

    barrier = pltpu.get_barrier_semaphore()
    for offset in range(1, n):
        pl.semaphore_signal(barrier, inc=1, device_id={"ga": peer(offset)}, device_id_type=MESH)
    for offset in range(1, n_pb):
        pl.semaphore_signal(barrier, inc=1, device_id={"pb": pb_peer(offset)}, device_id_type=MESH)
    pl.semaphore_wait(barrier, n - 1 + n_pb - 1)

    def is_target(device):
        return jnp.logical_and(device >= base, device < base + half)

    def set_of(device, i):
        return 2 * (device - base) + i // nk

    def hop(src, source, target, k, step):
        here = (source, target, pl.ds(k * vg, vg))
        return pltpu.make_async_remote_copy(
            src_ref=mbuf.at[here] if src is None else src.at[target, pl.ds(k * vg, vg)],
            dst_ref=mbuf.at[here],
            send_sem=msend.at[source, target, k],
            recv_sem=mrecv.at[source, target, k],
            device_id={"ga": lax.rem(me + step + n, n)},
            device_id_type=MESH,
        )

    def lanes_of(h):
        return pl.ds(pl.multiple_of(h * g_slab, g_slab), g_slab)

    def first_slab(chunk):
        return chunk * wc * n * NB // g_slab

    def last_slab(chunk):
        return ((chunk + 1) * wc * n * NB - 1) // g_slab

    def reaches_left(chunk, h, device):
        least = jnp.minimum(first_slab(chunk), h)
        most = jnp.maximum(first_slab(chunk), h)
        return jnp.where(jnp.logical_or(base == 0, device >= half), least, most) <= device

    def reaches_right(chunk, h, device):
        least = jnp.minimum(last_slab(chunk), h)
        most = jnp.maximum(last_slab(chunk), h)
        return jnp.where(jnp.logical_and(base == 0, device >= half), least, most) >= device

    def w_copy(source, chunk, h, step):
        slot = source if step < 0 else jnp.where(source == me, n, source)
        piece = chunk * n + h
        here = (pl.ds(chunk * wc, wc), source, slice(None), lanes_of(h))
        return pltpu.make_async_remote_copy(
            src_ref=wbuf.at[here],
            dst_ref=wbuf.at[here],
            send_sem=wsend.at[slot, piece],
            recv_sem=wrecv.at[source, piece],
            device_id={"ga": lax.rem(me + step + n, n)},
            device_id_type=MESH,
        )

    def goes_left(chunk, h):
        return jnp.logical_and(me > 0, reaches_left(chunk, h, me - 1))

    def goes_right(chunk, h):
        return jnp.logical_and(me < n - 1, reaches_right(chunk, h, me + 1))

    def send_elements(reach, i):
        k = lax.rem(i, nk)

        @pl.when(jnp.logical_and(me - reach >= 0, is_target(me - reach)))
        def _():
            hop(elements, me, set_of(me - reach, i), k, -1).start()

        @pl.when(jnp.logical_and(me + reach < n, is_target(me + reach)))
        def _():
            hop(elements, me, set_of(me + reach, i), k, 1).start()

    def first_elements(i, carry):
        send_elements(n - 1 - i, 0)
        return carry

    def more_elements(i, carry):
        send_elements(n - 1 - i // (span - 1), 1 + lax.rem(i, span - 1))
        return carry

    lax.fori_loop(0, n - 1, first_elements, 0)
    own_w.wait()
    count = counts[0]
    column = lax.broadcasted_iota(jnp.int32, (NB, g_total), 1)
    row = lax.broadcasted_iota(jnp.int32, (NB, g_total), 0)

    for chunk in range(nc):

        def mask_block(c, carry):
            g = row + (c * n + me) * NB
            inside = jnp.logical_and(g < count, column < count)
            block = wown[c].astype(jnp.float32)
            wbuf[c, me] = jnp.where(inside, block, 0.0).astype(jnp.bfloat16)
            return carry

        lax.fori_loop(chunk * wc, (chunk + 1) * wc, mask_block, 0)

        def send_own(h, carry):
            @pl.when(goes_left(chunk, h))
            def _():
                w_copy(me, chunk, h, -1).start()

            @pl.when(goes_right(chunk, h))
            def _():
                w_copy(me, chunk, h, 1).start()

            return carry

        lax.fori_loop(0, n, send_own, 0)

    own_m.wait()
    own_occ.wait()
    k_points = lax.broadcasted_iota(jnp.int32, occ.shape, 1)
    chosen = jnp.where(k_points == k_minus_q[0], occ[...], 0.0)
    weights[...] = jnp.broadcast_to(jnp.sum(chosen, axis=1, keepdims=True), weights.shape)
    acc[...] = jnp.zeros_like(acc)

    def w_block(g, h):
        if n_cycles % n == 0:
            cycles = n_cycles // n
            block = wbuf[pl.ds(g * cycles, cycles), :, :, lanes_of(h)]
        else:
            per_cycle = n * NB // g_slab
            start = lax.rem(g, per_cycle) * (g_slab // NB)
            block = wbuf[g // per_cycle, pl.ds(start, g_slab // NB), :, lanes_of(h)]
        return block.reshape(g_slab, g_slab)

    far = jnp.where(2 * me < n, n - 1, 0)

    def bands(d, first, size, part=None):
        t = base + d // 2
        pair[...] = jnp.zeros_like(pair)

        def column_slab(h, carry):
            low = jnp.where(t > me, jnp.where(h == me, 0, me), jnp.where(t == me, jnp.where(h < me, me, 0), me))
            above = jnp.where(h > me, 0, me + 1)
            middle = jnp.where(h > me, me + 1, n)
            below = jnp.where(h == me, n, jnp.where(h > me, me + 1, 0))
            end = jnp.where(t > me, above, jnp.where(t == me, middle, below))
            if part == "near":
                low = jnp.where(far == 0, jnp.maximum(low, 1), low)
                end = jnp.where(h == far, 0, jnp.where(far == 0, end, jnp.minimum(end, n - 1)))
            if part == "far":
                has_far = jnp.logical_and(low <= far, far < end)
                low = jnp.where(h == far, low, far)
                end = jnp.where(h == far, end, jnp.where(has_far, far + 1, 0))

            @pl.when(low < end)
            def _():
                prod[0 : size * n_state] = jnp.zeros((size * n_state, g_slab), jnp.float32)

                def row_slab(g, inner):
                    left = mbuf[g, d, pl.ds(first, size)].reshape(size * n_state, g_slab)
                    prod[0 : size * n_state] += jnp.dot(
                        left, w_block(g, h), preferred_element_type=jnp.float32
                    )
                    return inner

                lax.fori_loop(low, end, row_slab, 0)
                for v in range(size):
                    exact = prod[v * n_state : (v + 1) * n_state]
                    high_part = exact.astype(jnp.bfloat16)
                    low_part = (exact - high_part.astype(jnp.float32)).astype(jnp.bfloat16)
                    both = lax.dot_general(
                        jnp.concatenate([high_part, low_part], axis=0),
                        mbuf[h, d, first + v],
                        (((1,), (1,)), ((), ())),
                        preferred_element_type=jnp.float32,
                    )
                    pair[v] += both[:n_state] + both[n_state:]

            return carry

        lax.fori_loop(0, n, column_slab, 0)
        for v in range(size):
            weight = weights[pl.ds(d * v_per + first + v, 1), 0:n_state]
            acc[...] -= weight * pair[v]

    def w_round(distance, carry):
        low = me - distance
        high = me + distance

        def pass_w(i, inner):
            chunk = i // n
            h = lax.rem(i, n)

            @pl.when(jnp.logical_and(low >= 0, reaches_right(chunk, h, me)))
            def _():
                w_copy(low, chunk, h, 1).wait_recv()

                @pl.when(goes_right(chunk, h))
                def _():
                    w_copy(low, chunk, h, 1).start()

            @pl.when(jnp.logical_and(high < n, reaches_left(chunk, h, me)))
            def _():
                w_copy(high, chunk, h, -1).wait_recv()

                @pl.when(goes_left(chunk, h))
                def _():
                    w_copy(high, chunk, h, -1).start()

            return inner

        lax.fori_loop(0, nc * n, pass_w, 0)
        return carry

    total_more = (n - 1) * (span - 1)

    def w_and_elements(distance, carry):
        share = (total_more + n - 2) // (n - 1)
        start = (distance - 1) * share
        lax.fori_loop(start, jnp.minimum(start + share, total_more), more_elements, 0)
        return w_round(distance, carry)

    lax.fori_loop(1, n, w_and_elements, 0)

    def round_of(distance, carry):
        low = me - distance
        high = me + distance

        def pass_m(i, inner):
            reach = n - 1 - i // span
            j = lax.rem(i, span)
            k = lax.rem(j, nk)
            right = me + reach
            left = me - reach
            right_ok = jnp.logical_and(right < n, is_target(right))
            left_ok = jnp.logical_and(left >= 0, is_target(left))

            @pl.when(jnp.logical_and(low >= 0, right_ok))
            def _():
                hop(None, low, set_of(right, j), k, 1).wait_recv()
                hop(None, low, set_of(right, j), k, 1).start()

            @pl.when(jnp.logical_and(high < n, left_ok))
            def _():
                hop(None, high, set_of(left, j), k, -1).wait_recv()
                hop(None, high, set_of(left, j), k, -1).start()

            group_ends = lax.rem(k, group) == group - 1
            first = (k - (group - 1)) * vg
            to_right = jnp.logical_and(right_ok, distance == jnp.maximum(me, 1))
            to_left = jnp.logical_and(left_ok, distance == jnp.maximum(n - 1 - me, 1))

            def side(which, most):
                d = jnp.where(which == 0, set_of(right, j), set_of(left, j))
                wanted = jnp.logical_or(
                    jnp.logical_and(which == 0, to_right), jnp.logical_and(which == 1, to_left)
                )

                @pl.when(jnp.logical_and(group_ends, wanted))
                def _():
                    bands(d, first, group * vg)

                return most

            lax.fori_loop(0, 2, side, 0)
            return inner

        lax.fori_loop(0, (n - 1) * span, pass_m, 0)
        return carry

    lax.fori_loop(1, n, round_of, 0)

    def arrived(d, k, is_far):
        for source in range(n):

            @pl.when(jnp.logical_and(source != me, (far == source) == is_far))
            def _():
                hop(None, source, d, k, 1).wait_recv()

    def near_group(i, carry):
        d = set_of(me, i * group)
        k = lax.rem(i * group, nk)
        for j in range(group):
            arrived(d, k + j, False)
        bands(d, k * vg, group * vg, "near")
        return carry

    def far_group(i, carry):
        d = set_of(me, i)
        k = lax.rem(i, nk)
        arrived(d, k, True)
        bands(d, k * vg, vg, "far")
        return carry

    @pl.when(is_target(me))
    def _():
        lax.fori_loop(0, span // group, near_group, 0)
        lax.fori_loop(0, span, far_group, 0)

    def g_copy(offset):
        return pltpu.make_async_remote_copy(
            src_ref=parts.at[peer(offset)],
            dst_ref=ga_in.at[me],
            send_sem=gsend.at[offset - 1],
            recv_sem=grecv.at[offset - 1],
            device_id={"ga": peer(offset)},
            device_id_type=MESH,
        )

    parts[...] = jnp.zeros_like(parts)
    for j in range(n):
        parts[j, 0:rows, 0:n_state] = acc[j * rows : (j + 1) * rows, :]
    for offset in range(1, n):
        g_copy(offset).start()
    ga_in[me] = parts[me]
    for offset in range(1, n):
        g_copy(offset).wait_recv()
    total = ga_in[0]
    for j in range(1, n):
        total = total + ga_in[j]
    pb_in[my_pb] = total

    def p_copy(offset):
        return pltpu.make_async_remote_copy(
            src_ref=pb_in.at[my_pb],
            dst_ref=pb_in.at[my_pb],
            send_sem=psend.at[offset - 1],
            recv_sem=precv.at[offset - 1],
            device_id={"pb": pb_peer(offset)},
            device_id_type=MESH,
        )

    for offset in range(1, n_pb):
        p_copy(offset).start()
    for offset in range(1, n_pb):
        p_copy(offset).wait_recv()
    result = pb_in[0]
    for j in range(1, n_pb):
        result = result + pb_in[j]
    out[...] = result[0:rows, 0:n_state]

    for offset in range(1, n_pb):
        p_copy(offset).wait_send()
    for offset in range(1, n):
        g_copy(offset).wait_send()

    def sent_elements(i, carry):
        source = i // (n * nk)
        d = lax.rem(i // nk, n)
        target = base + d // 2
        k = lax.rem(i, nk)

        @pl.when(jnp.logical_and(source == me, target != me))
        def _():
            hop(elements, source, d, k, 1).wait_send()

        passed = jnp.logical_or(
            jnp.logical_and(source < me, target > me), jnp.logical_and(source > me, target < me)
        )

        @pl.when(passed)
        def _():
            hop(None, source, d, k, 1).wait_send()

        return carry

    lax.fori_loop(0, n * n * nk, sent_elements, 0)

    def sent_pieces(i, carry):
        source = i // (nc * n)
        chunk = lax.rem(i // n, nc)
        h = lax.rem(i, n)

        @pl.when(jnp.logical_and(source >= me, goes_left(chunk, h)))
        def _():
            w_copy(source, chunk, h, -1).wait_send()

        @pl.when(jnp.logical_and(source <= me, goes_right(chunk, h)))
        def _():
            w_copy(source, chunk, h, 1).wait_send()

        return carry

    lax.fori_loop(0, n * nc * n, sent_pieces, 0)


def on_device(n, n_pb, elements, screened, counts, k_minus_q, occupation):
    _, n_band, n_state, g_slab = elements.shape
    g_total = screened.shape[2]
    v_per = n_band // n
    n_cycles = g_slab // NB
    vg = 2 if v_per % 4 == 0 else 1
    nc = min(4, n_cycles)
    wc = n_cycles // nc
    nk = v_per // vg
    group = 2 if nk % 2 == 0 else 1
    rows = n_state // n
    padded = (rows + 7) // 8 * 8
    lanes = (n_state + 127) // 128 * 128
    any_spec = pl.BlockSpec(memory_space=pl.ANY)
    smem = pl.BlockSpec(memory_space=pltpu.SMEM)
    vmem = pl.BlockSpec(memory_space=pltpu.VMEM)
    dma = pltpu.SemaphoreType.DMA
    return pl.pallas_call(
        functools.partial(kernel, n, n_pb, vg, wc),
        out_shape=jax.ShapeDtypeStruct((rows, n_state), jnp.float32),
        in_specs=[any_spec, any_spec, smem, smem, any_spec],
        out_specs=vmem,
        scratch_shapes=[
            pltpu.VMEM((n, n, v_per, n_state, g_slab), jnp.bfloat16),
            pltpu.VMEM((n_cycles, n, NB, g_total), jnp.bfloat16),
            pltpu.VMEM((n_cycles, NB, g_total), jnp.bfloat16),
            pltpu.VMEM(occupation.shape[::-1], jnp.float32),
            pltpu.VMEM((n_band, lanes), jnp.float32),
            pltpu.VMEM((group * vg * n_state, g_slab), jnp.float32),
            pltpu.VMEM((group * vg, n_state, n_state), jnp.float32),
            pltpu.VMEM((n_state, n_state), jnp.float32),
            pltpu.VMEM((n, padded, lanes), jnp.float32),
            pltpu.VMEM((n, padded, lanes), jnp.float32),
            pltpu.VMEM((n_pb, padded, lanes), jnp.float32),
            dma((3,)),
            dma((n + 1, nc * n)),
            dma((n, nc * n)),
            dma((n, n, nk)),
            dma((n, n, nk)),
            dma((n - 1,)),
            dma((n - 1,)),
            dma((n_pb - 1,)),
            dma((n_pb - 1,)),
        ],
        compiler_params=pltpu.CompilerParams(
            collective_id=0, has_side_effects=True, vmem_limit_bytes=56 * 1024 * 1024
        ),
        cost_estimate=pl.CostEstimate(
            flops=2 * v_per * n_state * g_total * (g_total + n_state),
            bytes_accessed=16 * 1024 * 1024,
            transcendentals=0,
        ),
    )(
        elements.reshape(n, v_per, n_state, g_slab),
        screened.reshape(n_cycles, NB, g_total),
        counts,
        k_minus_q,
        occupation.T,
    )


def solution(mesh):
    return jax.shard_map(
        functools.partial(on_device, mesh.shape["ga"], mesh.shape["pb"]),
        mesh=mesh,
        in_specs=(P("pb", None, None, "ga"), P("pb", "ga", None), P("pb"), P("pb"), P()),
        out_specs=P("ga", None),
        check_vma=False,
    )
```

```python
import functools

import jax
import jax.numpy as jnp
from jax import lax
from jax.experimental import pallas as pl
from jax.experimental.pallas import tpu as pltpu
from jax.sharding import PartitionSpec as P

NB = 32
MESH = pl.DeviceIdType.MESH


def kernel(
    n, n_pb, vg, wc,
    elements, screened, counts, k_minus_q, occupation, out,
    mbuf, wbuf, wown, occ, weights, prod, pair, acc, parts, ga_in, pb_in,
    local_sem, wsend, wrecv, msend, mrecv, gsend, grecv, psend, precv,
):
    me = lax.axis_index("ga")
    my_pb = lax.axis_index("pb")
    _, v_per, n_state, g_slab = elements.shape
    n_cycles, _, g_total = screened.shape
    rows = n_state // n
    nk = v_per // vg
    nc = n_cycles // wc
    group = 2 if nk % 2 == 0 else 1

    def peer(offset):
        return lax.rem(me + offset, n)

    def pb_peer(offset):
        return lax.rem(my_pb + offset, n_pb)

    own_w = pltpu.make_async_copy(screened, wown, local_sem.at[0])
    own_m = pltpu.make_async_copy(elements, mbuf.at[me], local_sem.at[1])
    own_occ = pltpu.make_async_copy(occupation, occ, local_sem.at[2])
    own_w.start()
    own_m.start()
    own_occ.start()

    barrier = pltpu.get_barrier_semaphore()
    for offset in range(1, n):
        pl.semaphore_signal(barrier, inc=1, device_id={"ga": peer(offset)}, device_id_type=MESH)
    for offset in range(1, n_pb):
        pl.semaphore_signal(barrier, inc=1, device_id={"pb": pb_peer(offset)}, device_id_type=MESH)
    pl.semaphore_wait(barrier, n - 1 + n_pb - 1)

    def hop(src, source, target, k, step):
        here = (source, target, pl.ds(k * vg, vg))
        return pltpu.make_async_remote_copy(
            src_ref=mbuf.at[here] if src is None else src.at[target, pl.ds(k * vg, vg)],
            dst_ref=mbuf.at[here],
            send_sem=msend.at[source, target, k],
            recv_sem=mrecv.at[source, target, k],
            device_id={"ga": lax.rem(me + step + n, n)},
            device_id_type=MESH,
        )

    def lanes_of(h):
        return pl.ds(pl.multiple_of(h * g_slab, g_slab), g_slab)

    def first_slab(chunk):
        return chunk * wc * n * NB // g_slab

    def last_slab(chunk):
        return ((chunk + 1) * wc * n * NB - 1) // g_slab

    def reaches_left(chunk, h, device):
        return jnp.logical_or(first_slab(chunk) <= device, h <= device)

    def reaches_right(chunk, h, device):
        return jnp.logical_or(last_slab(chunk) >= device, h >= device)

    def w_copy(source, chunk, h, step):
        slot = source if step < 0 else jnp.where(source == me, n, source)
        piece = chunk * n + h
        here = (pl.ds(chunk * wc, wc), source, slice(None), lanes_of(h))
        return pltpu.make_async_remote_copy(
            src_ref=wbuf.at[here],
            dst_ref=wbuf.at[here],
            send_sem=wsend.at[slot, piece],
            recv_sem=wrecv.at[source, piece],
            device_id={"ga": lax.rem(me + step + n, n)},
            device_id_type=MESH,
        )

    def goes_left(chunk, h):
        return jnp.logical_and(me > 0, reaches_left(chunk, h, me - 1))

    def goes_right(chunk, h):
        return jnp.logical_and(me < n - 1, reaches_right(chunk, h, me + 1))

    def send_elements(reach, k):
        @pl.when(me - reach >= 0)
        def _():
            hop(elements, me, me - reach, k, -1).start()

        @pl.when(me + reach < n)
        def _():
            hop(elements, me, me + reach, k, 1).start()

    def first_elements(i, carry):
        send_elements(n - 1 - i, 0)
        return carry

    def more_elements(i, carry):
        send_elements(n - 1 - i // (nk - 1), 1 + lax.rem(i, nk - 1))
        return carry

    lax.fori_loop(0, n - 1, first_elements, 0)
    own_w.wait()
    count = counts[0]
    column = lax.broadcasted_iota(jnp.int32, (NB, g_total), 1)
    row = lax.broadcasted_iota(jnp.int32, (NB, g_total), 0)

    for chunk in range(nc):

        def mask_block(c, carry):
            g = row + (c * n + me) * NB
            inside = jnp.logical_and(g < count, column < count)
            block = wown[c].astype(jnp.float32)
            wbuf[c, me] = jnp.where(inside, block, 0.0).astype(jnp.bfloat16)
            return carry

        lax.fori_loop(chunk * wc, (chunk + 1) * wc, mask_block, 0)

        def send_own(h, carry):
            @pl.when(goes_left(chunk, h))
            def _():
                w_copy(me, chunk, h, -1).start()

            @pl.when(goes_right(chunk, h))
            def _():
                w_copy(me, chunk, h, 1).start()

            return carry

        lax.fori_loop(0, n, send_own, 0)

    own_m.wait()
    own_occ.wait()
    k_points = lax.broadcasted_iota(jnp.int32, occ.shape, 1)
    chosen = jnp.where(k_points == k_minus_q[0], occ[...], 0.0)
    weights[...] = jnp.broadcast_to(jnp.sum(chosen, axis=1, keepdims=True), weights.shape)
    acc[...] = jnp.zeros_like(acc)

    def w_block(g, h):
        if n_cycles % n == 0:
            cycles = n_cycles // n
            block = wbuf[pl.ds(g * cycles, cycles), :, :, lanes_of(h)]
        else:
            per_cycle = n * NB // g_slab
            start = lax.rem(g, per_cycle) * (g_slab // NB)
            block = wbuf[g // per_cycle, pl.ds(start, g_slab // NB), :, lanes_of(h)]
        return block.reshape(g_slab, g_slab)

    far = jnp.where(2 * me < n, n - 1, 0)

    def bands(d, first, size, part=None):
        pair[...] = jnp.zeros_like(pair)

        def column_slab(h, carry):
            low = jnp.where(d > me, jnp.where(h == me, 0, me), jnp.where(d == me, jnp.where(h < me, me, 0), me))
            above = jnp.where(h > me, 0, me + 1)
            middle = jnp.where(h > me, me + 1, n)
            below = jnp.where(h == me, n, jnp.where(h > me, me + 1, 0))
            end = jnp.where(d > me, above, jnp.where(d == me, middle, below))
            if part == "near":
                low = jnp.where(far == 0, jnp.maximum(low, 1), low)
                end = jnp.where(h == far, 0, jnp.where(far == 0, end, jnp.minimum(end, n - 1)))
            if part == "far":
                has_far = jnp.logical_and(low <= far, far < end)
                low = jnp.where(h == far, low, far)
                end = jnp.where(h == far, end, jnp.where(has_far, far + 1, 0))

            @pl.when(low < end)
            def _():
                prod[0 : size * n_state] = jnp.zeros((size * n_state, g_slab), jnp.float32)

                def row_slab(g, inner):
                    left = mbuf[g, d, pl.ds(first, size)].reshape(size * n_state, g_slab)
                    prod[0 : size * n_state] += jnp.dot(
                        left, w_block(g, h), preferred_element_type=jnp.float32
                    )
                    return inner

                lax.fori_loop(low, end, row_slab, 0)
                for v in range(size):
                    exact = prod[v * n_state : (v + 1) * n_state]
                    high_part = exact.astype(jnp.bfloat16)
                    low_part = (exact - high_part.astype(jnp.float32)).astype(jnp.bfloat16)
                    both = lax.dot_general(
                        jnp.concatenate([high_part, low_part], axis=0),
                        mbuf[h, d, first + v],
                        (((1,), (1,)), ((), ())),
                        preferred_element_type=jnp.float32,
                    )
                    pair[v] += both[:n_state] + both[n_state:]

            return carry

        lax.fori_loop(0, n, column_slab, 0)
        for v in range(size):
            weight = weights[pl.ds(d * v_per + first + v, 1), 0:n_state]
            acc[...] -= weight * pair[v]

    def w_round(distance, carry):
        low = me - distance
        high = me + distance

        def pass_w(i, inner):
            chunk = i // n
            h = lax.rem(i, n)

            @pl.when(jnp.logical_and(low >= 0, reaches_right(chunk, h, me)))
            def _():
                w_copy(low, chunk, h, 1).wait_recv()

                @pl.when(goes_right(chunk, h))
                def _():
                    w_copy(low, chunk, h, 1).start()

            @pl.when(jnp.logical_and(high < n, reaches_left(chunk, h, me)))
            def _():
                w_copy(high, chunk, h, -1).wait_recv()

                @pl.when(goes_left(chunk, h))
                def _():
                    w_copy(high, chunk, h, -1).start()

            return inner

        lax.fori_loop(0, nc * n, pass_w, 0)
        return carry

    total_more = (n - 1) * (nk - 1)

    def w_and_elements(distance, carry):
        share = (total_more + n - 2) // (n - 1)
        start = (distance - 1) * share
        lax.fori_loop(start, jnp.minimum(start + share, total_more), more_elements, 0)
        return w_round(distance, carry)

    lax.fori_loop(1, n, w_and_elements, 0)

    def round_of(distance, carry):
        low = me - distance
        high = me + distance

        def pass_m(i, inner):
            reach = n - 1 - i // nk
            k = lax.rem(i, nk)

            @pl.when(jnp.logical_and(low >= 0, me + reach < n))
            def _():
                hop(None, low, me + reach, k, 1).wait_recv()
                hop(None, low, me + reach, k, 1).start()

            @pl.when(jnp.logical_and(high < n, me - reach >= 0))
            def _():
                hop(None, high, me - reach, k, -1).wait_recv()
                hop(None, high, me - reach, k, -1).start()

            group_ends = lax.rem(k, group) == group - 1
            first = (k - (group - 1)) * vg
            to_right = jnp.logical_and(me + reach < n, distance == jnp.maximum(me, 1))
            to_left = jnp.logical_and(me - reach >= 0, distance == jnp.maximum(n - 1 - me, 1))

            def side(j, most):
                d = jnp.where(j == 0, me + reach, me - reach)
                wanted = jnp.where(j == 0, to_right, to_left)

                @pl.when(jnp.logical_and(group_ends, wanted))
                def _():
                    bands(d, first, group * vg)

                return most

            lax.fori_loop(0, 2, side, 0)
            return inner

        lax.fori_loop(0, (n - 1) * nk, pass_m, 0)
        return carry

    lax.fori_loop(1, n, round_of, 0)

    def arrived(k, is_far):
        for source in range(n):

            @pl.when(jnp.logical_and(source != me, (far == source) == is_far))
            def _():
                hop(None, source, me, k, 1).wait_recv()

    def near_group(i, carry):
        for j in range(group):
            arrived(i * group + j, False)
        bands(me, i * group * vg, group * vg, "near")
        return carry

    lax.fori_loop(0, nk // group, near_group, 0)

    def far_group(k, carry):
        arrived(k, True)
        bands(me, k * vg, vg, "far")
        return carry

    lax.fori_loop(0, nk, far_group, 0)

    def g_copy(offset):
        return pltpu.make_async_remote_copy(
            src_ref=parts.at[peer(offset)],
            dst_ref=ga_in.at[me],
            send_sem=gsend.at[offset - 1],
            recv_sem=grecv.at[offset - 1],
            device_id={"ga": peer(offset)},
            device_id_type=MESH,
        )

    parts[...] = jnp.zeros_like(parts)
    for j in range(n):
        parts[j, 0:rows, 0:n_state] = acc[j * rows : (j + 1) * rows, :]
    for offset in range(1, n):
        g_copy(offset).start()
    ga_in[me] = parts[me]
    for offset in range(1, n):
        g_copy(offset).wait_recv()
    total = ga_in[0]
    for j in range(1, n):
        total = total + ga_in[j]
    pb_in[my_pb] = total

    def p_copy(offset):
        return pltpu.make_async_remote_copy(
            src_ref=pb_in.at[my_pb],
            dst_ref=pb_in.at[my_pb],
            send_sem=psend.at[offset - 1],
            recv_sem=precv.at[offset - 1],
            device_id={"pb": pb_peer(offset)},
            device_id_type=MESH,
        )

    for offset in range(1, n_pb):
        p_copy(offset).start()
    for offset in range(1, n_pb):
        p_copy(offset).wait_recv()
    result = pb_in[0]
    for j in range(1, n_pb):
        result = result + pb_in[j]
    out[...] = result[0:rows, 0:n_state]

    for offset in range(1, n_pb):
        p_copy(offset).wait_send()
    for offset in range(1, n):
        g_copy(offset).wait_send()

    def sent_elements(i, carry):
        source = i // (n * nk)
        target = lax.rem(i // nk, n)
        k = lax.rem(i, nk)

        @pl.when(jnp.logical_and(source == me, target != me))
        def _():
            hop(elements, source, target, k, 1).wait_send()

        passed = jnp.logical_or(
            jnp.logical_and(source < me, target > me), jnp.logical_and(source > me, target < me)
        )

        @pl.when(passed)
        def _():
            hop(None, source, target, k, 1).wait_send()

        return carry

    lax.fori_loop(0, n * n * nk, sent_elements, 0)

    def sent_pieces(i, carry):
        source = i // (nc * n)
        chunk = lax.rem(i // n, nc)
        h = lax.rem(i, n)

        @pl.when(jnp.logical_and(source >= me, goes_left(chunk, h)))
        def _():
            w_copy(source, chunk, h, -1).wait_send()

        @pl.when(jnp.logical_and(source <= me, goes_right(chunk, h)))
        def _():
            w_copy(source, chunk, h, 1).wait_send()

        return carry

    lax.fori_loop(0, n * nc * n, sent_pieces, 0)


def on_device(n, n_pb, elements, screened, counts, k_minus_q, occupation):
    _, n_band, n_state, g_slab = elements.shape
    g_total = screened.shape[2]
    v_per = n_band // n
    n_cycles = g_slab // NB
    vg = 4 if v_per % 8 == 0 else 2 if v_per % 4 == 0 else 1
    nc = min(4, n_cycles)
    wc = n_cycles // nc
    nk = v_per // vg
    group = 2 if nk % 2 == 0 else 1
    rows = n_state // n
    padded = (rows + 7) // 8 * 8
    lanes = (n_state + 127) // 128 * 128
    any_spec = pl.BlockSpec(memory_space=pl.ANY)
    smem = pl.BlockSpec(memory_space=pltpu.SMEM)
    vmem = pl.BlockSpec(memory_space=pltpu.VMEM)
    dma = pltpu.SemaphoreType.DMA
    return pl.pallas_call(
        functools.partial(kernel, n, n_pb, vg, wc),
        out_shape=jax.ShapeDtypeStruct((rows, n_state), jnp.float32),
        in_specs=[any_spec, any_spec, smem, smem, any_spec],
        out_specs=vmem,
        scratch_shapes=[
            pltpu.VMEM((n, n, v_per, n_state, g_slab), jnp.bfloat16),
            pltpu.VMEM((n_cycles, n, NB, g_total), jnp.bfloat16),
            pltpu.VMEM((n_cycles, NB, g_total), jnp.bfloat16),
            pltpu.VMEM(occupation.shape[::-1], jnp.float32),
            pltpu.VMEM((n_band, lanes), jnp.float32),
            pltpu.VMEM((group * vg * n_state, g_slab), jnp.float32),
            pltpu.VMEM((group * vg, n_state, n_state), jnp.float32),
            pltpu.VMEM((n_state, n_state), jnp.float32),
            pltpu.VMEM((n, padded, lanes), jnp.float32),
            pltpu.VMEM((n, padded, lanes), jnp.float32),
            pltpu.VMEM((n_pb, padded, lanes), jnp.float32),
            dma((3,)),
            dma((n + 1, nc * n)),
            dma((n, nc * n)),
            dma((n, n, nk)),
            dma((n, n, nk)),
            dma((n - 1,)),
            dma((n - 1,)),
            dma((n_pb - 1,)),
            dma((n_pb - 1,)),
        ],
        compiler_params=pltpu.CompilerParams(
            collective_id=0, has_side_effects=True, vmem_limit_bytes=56 * 1024 * 1024
        ),
        cost_estimate=pl.CostEstimate(
            flops=2 * v_per * n_state * g_total * (g_total + n_state),
            bytes_accessed=16 * 1024 * 1024,
            transcendentals=0,
        ),
    )(
        elements.reshape(n, v_per, n_state, g_slab),
        screened.reshape(n_cycles, NB, g_total),
        counts,
        k_minus_q,
        occupation.T,
    )


def solution(mesh):
    return jax.shard_map(
        functools.partial(on_device, mesh.shape["ga"], mesh.shape["pb"]),
        mesh=mesh,
        in_specs=(P("pb", None, None, "ga"), P("pb", "ga", None), P("pb"), P("pb"), P()),
        out_specs=P("ga", None),
        check_vma=False,
    )
```
